256 devices in a mesh: prow: 16 (over z_hi, y), pcol: 16 (over z_lo, x, core).
Axes of the slice: x: 4, y: 4, z: 8 (z_hi: 4, z_lo: 2; z = z_hi * 2 + z_lo), core: 2. Of those that a mesh axis runs over, the one named last changes fastest.
Arguments:
- top_inverse: float32 [8192, 8192], P('prow', 'pcol'), as said below
- panel_one: float32 [2560, 4096], P('prow', 'pcol'), may hold values from -0.125 to 0.125
- panel_two: float32 [1280, 8192], P('prow', 'pcol'), may hold values from -0.15625 to 0.15625
- parent_rows: float32 [256, 8192], P('prow', 'pcol'), may hold values from -0.15625 to 0.15625
- pivot_one: float32 [256, 4096], P('prow', 'pcol'), as said below
- pivot_two: float32 [256, 8192], P('prow', 'pcol'), as said below
- sets_one: int32 [16, 10], replicated, may hold values from 0 to 31, as said below
- sets_two: int32 [32, 5], replicated, may hold values from 0 to 31, as said below
Outputs:
- below_one: float32 [2560, 4096], P('prow', 'pcol')
- corner_one: float32 [256, 4096], P('prow', 'pcol')
- below_two: float32 [1280, 8192], P('prow', 'pcol')
- beside_two: float32 [256, 8192], P('prow', 'pcol')
- corner_two: float32 [256, 8192], P('prow', 'pcol')
The draws below stay inside these ranges and needn't reach their ends.
Inputs may be any that keep to these rules, and one draw needn't show every extreme that they name: top_inverse is symmetric. `pivot_one`: every 256 x 256 column block is symmetric. `pivot_two`: every 256 x 256 column block is symmetric. `sets_one`: each row holds 10 different ancestor supernodes in increasing order. `sets_two`: row C holds 5 different entries of row C // 2 of sets_one, in increasing order.
All inputs are finite; a program needn't handle non-finite values.
Results may differ from the reference program's by a relative error of at most 0.0003.
Values sent between devices are 32-bit elements; how exact they have to be, the bound alone decides.
A program may use at most 128 MiB of HBM per device.

```python
import jax
import jax.numpy as jnp
from jax import lax

B = 256
NB = 32
S1 = 10
S2 = 5
K1 = 16
K2 = 32
N = 8192


def structure_sets(key):
    scores = jax.random.randint(key, (K1, NB), 0, 1 << 20) * NB + jnp.arange(NB, dtype=jnp.int32)[None, :]
    order = jnp.argsort(scores, axis=1).astype(jnp.int32)
    return jnp.sort(order[:, :S1], axis=1).astype(jnp.int32)


def symmetric_blocks(key, count, noise):
    key_diag = jax.random.fold_in(key, 5)
    twin = (noise + jnp.transpose(noise, (2, 1, 0))) * 0.35
    values = jax.random.uniform(key_diag, (count, B), jnp.float32, 1.0, 3.0)
    eye = (jnp.arange(B)[:, None] == jnp.arange(B)[None, :]).astype(jnp.float32)
    return (twin + eye[:, None, :] * values[None, :, :]).reshape(B, count * B)


def draw_top_inverse(key, part):
    key = jax.random.fold_in(key, 11)
    key_noise, key_diag = jax.random.split(key)
    noise = jax.random.normal(key_noise, (N, N), jnp.float32)
    twin = (noise + noise.T) * 0.045
    values = jax.random.uniform(key_diag, (N,), jnp.float32, 4.0, 8.0)
    eye = (jnp.arange(N)[:, None] == jnp.arange(N)[None, :]).astype(jnp.float32)
    return twin + eye * values[None, :]


def draw_pivot_one(key, part):
    key = jax.random.fold_in(key, 21)
    noise = jax.random.normal(key, (B, K1, B), jnp.float32)
    return symmetric_blocks(key, K1, noise)


def draw_pivot_two(key, part):
    key = jax.random.fold_in(key, 31)
    noise = jax.random.normal(key, (B, K2, B), jnp.float32)
    return symmetric_blocks(key, K2, noise)


def draw_sets_one(key, part):
    shared = structure_sets(key)
    return shared


def draw_sets_two(key, part):
    shared = structure_sets(key)
    key = jax.random.fold_in(key, 41)
    scores = jax.random.randint(key, (K2, S1), 0, 1 << 20) * S1 + jnp.arange(S1, dtype=jnp.int32)[None, :]
    picks = jnp.sort(jnp.argsort(scores, axis=1)[:, :S2].astype(jnp.int32), axis=1)
    parents = shared[jnp.arange(K2, dtype=jnp.int32) // 2]
    chosen = jnp.take_along_axis(parents, picks, axis=1)
    return jnp.sort(chosen, axis=1).astype(jnp.int32)


def steps_of(own_key, shape, shards, smallest, top_value):
    factor_of = 1.0
    for dim, shards_of in shards:
        heights = jax.random.uniform(jax.random.fold_in(jax.random.fold_in(own_key, 6), dim), (shards_of,), jnp.float32, smallest / len(shards), top_value / len(shards))
        factor_of = factor_of * jnp.repeat(jnp.exp(heights), shape[dim] // shards_of).reshape((-1,) + (1,) * (len(shape) - 1 - dim))
    return factor_of


def centred(stream_key, extent, spread, most, pieces=(), held_as=jnp.bfloat16):
    result = jax.random.normal(stream_key, extent, jnp.float32) * spread
    if len(pieces) > 0:
        result = steps_of(stream_key, extent, pieces, -0.22, 0.18) * result
    return jnp.clip(result, min=-most, max=most).astype(held_as)


def setup_inputs(seed: int = 0) -> dict:
    streams_of = jax.random.split(jax.random.key(seed), 9)
    return {
        "top_inverse": draw_top_inverse(jax.random.fold_in(streams_of[8], 71), 0),
        "panel_one": centred(streams_of[1], (S1 * B, K1 * B), (S1 * B) ** -0.5, 0.125, ((0, 16), (1, 16)), jnp.float32),
        "panel_two": centred(streams_of[2], (S2 * B, K2 * B), ((S2 + 1) * B) ** -0.5, 0.15625, ((0, 16), (1, 16)), jnp.float32),
        "parent_rows": centred(streams_of[3], (B, K2 * B), ((S2 + 1) * B) ** -0.5, 0.15625, ((0, 16), (1, 16)), jnp.float32),
        "pivot_one": draw_pivot_one(jax.random.fold_in(streams_of[8], 71), 0),
        "pivot_two": draw_pivot_two(jax.random.fold_in(streams_of[8], 71), 0),
        "sets_one": draw_sets_one(jax.random.fold_in(streams_of[8], 71), 0),
        "sets_two": draw_sets_two(jax.random.fold_in(streams_of[8], 71), 0),
    }


EXACT = lax.Precision.HIGHEST


def pick_blocks(top_blocks, sets):
    count = sets.shape[0]
    rows = jnp.take(top_blocks, sets, axis=0)
    grid = jnp.take(rows, sets, axis=2)
    return grid.reshape(count * B, count * B)


def by_column(values, rows, count):
    return values.reshape(rows, count, B).transpose(1, 0, 2)


def reference(top_inverse, panel_one, panel_two, parent_rows, pivot_one, pivot_two, sets_one, sets_two):
    top_blocks = top_inverse.reshape(NB, B, NB, B)
    low_one_s = by_column(panel_one, S1 * B, K1)
    pivot_one_s = by_column(pivot_one, B, K1)
    low_two_s = by_column(panel_two, S2 * B, K2)
    parent_s = by_column(parent_rows, B, K2)
    pivot_two_s = by_column(pivot_two, B, K2)

    def level_one(inputs):
        sets, low, pivot = inputs
        grid = pick_blocks(top_blocks, sets)
        below = -jnp.dot(grid, low, precision=EXACT, preferred_element_type=jnp.float32)
        corner = pivot - jnp.dot(low.T, below, precision=EXACT, preferred_element_type=jnp.float32)
        return below, corner

    below_one_s, corner_one_s = lax.map(level_one, (sets_one, low_one_s, pivot_one_s))

    def level_two(inputs):
        child, sets, low, parent, pivot = inputs
        father = child // 2
        sets_father = sets_one[father]
        match = (sets[:, None] == sets_father[None, :]).astype(jnp.float32)
        upper = jnp.einsum("ts,sbe->tbe", match, below_one_s[father].reshape(S1, B, B), precision=EXACT).reshape(S2 * B, B)
        grid = pick_blocks(top_blocks, sets)
        direct = jnp.dot(grid, low, precision=EXACT, preferred_element_type=jnp.float32)
        couple = jnp.dot(upper, parent, precision=EXACT, preferred_element_type=jnp.float32)
        below = -(direct + couple)
        beside = -(jnp.dot(corner_one_s[father], parent, precision=EXACT, preferred_element_type=jnp.float32) + jnp.dot(upper.T, low, precision=EXACT, preferred_element_type=jnp.float32))
        first = jnp.dot(parent.T, beside, precision=EXACT, preferred_element_type=jnp.float32)
        second = jnp.dot(low.T, below, precision=EXACT, preferred_element_type=jnp.float32)
        return below, beside, pivot - first - second

    children = jnp.arange(K2, dtype=jnp.int32)
    below_two_s, beside_s, corner_two_s = lax.map(level_two, (children, sets_two, low_two_s, parent_s, pivot_two_s))
    below_one = below_one_s.transpose(1, 0, 2).reshape(S1 * B, K1 * B)
    corner_one = corner_one_s.transpose(1, 0, 2).reshape(B, K1 * B)
    below_two = below_two_s.transpose(1, 0, 2).reshape(S2 * B, K2 * B)
    beside_two = beside_s.transpose(1, 0, 2).reshape(B, K2 * B)
    corner_two = corner_two_s.transpose(1, 0, 2).reshape(B, K2 * B)
    return below_one, corner_one, below_two, beside_two, corner_two
```

```python
import functools

import jax
import jax.numpy as jnp
from jax import lax
from jax.experimental import pallas as pl
from jax.experimental.pallas import tpu as pltpu
from jax.sharding import PartitionSpec as P

MESH = pl.DeviceIdType.MESH
EXACT = lax.Precision.HIGHEST
F32 = jnp.float32


def mm(a, b):
    return jnp.dot(a, b, precision=EXACT, preferred_element_type=F32)


def mm_t(a, b):
    return lax.dot_general(
        a, b, (((0,), (0,)), ((), ())), precision=EXACT, preferred_element_type=F32
    )


def kernel(
    cfg,
    sets_one, sets_two, top, panel_one, panel_two, parent, pivot_one, pivot_two,
    below_one, corner_one, below_two, beside, corner_two,
    arows, zs, packed, landed, grid, l1, l2, pf,
    acc1, acc2, low1, low2, dir2, upper, b2s, part, sums, out1, out2,
    a_send, a_recv, b_send, b_recv, c_send, c_recv,
    g_send, g_recv, h_send, h_recv, own_sem, s_send, s_recv, o1_send, o1_recv, o2_send, o2_recv,
):
    nr, nc, ny, B, S1, S2 = cfg
    nz = nr // ny
    sub = B // nr
    H = max(B // 128, 1)
    LN = B // H
    r = lax.axis_index("prow")
    c = lax.axis_index("pcol")
    zi = r // ny
    yi = r % ny
    nbr = top.shape[0]
    npc = S1 * S1 * H
    rows1 = S1 * sub
    rows2 = S2 * sub

    def to_row(d):
        return (d, c)

    def to_col(d):
        return (r, d)

    def each(n, f):
        def body(k, _):
            f(k)
            return 0
        lax.fori_loop(0, n, body, 0)

    def rcopy(src, dst, ss, rs, dev):
        return pltpu.make_async_remote_copy(
            src_ref=src, dst_ref=dst, send_sem=ss, recv_sem=rs, device_id=dev, device_id_type=MESH
        )

    barrier = pltpu.get_barrier_semaphore()

    def greet_rows(k):
        pl.semaphore_signal(barrier, inc=1, device_id=to_row((r + k + 1) % nr), device_id_type=MESH)

    def greet_cols(k):
        pl.semaphore_signal(barrier, inc=1, device_id=to_col((c + k + 1) % nc), device_id_type=MESH)

    each(nr - 1, greet_rows)
    each(nc - 1, greet_cols)
    pl.semaphore_wait(barrier, nr + nc - 2)

    own = [
        pltpu.make_async_copy(panel_one, l1.at[pl.ds(r * rows1, rows1)], own_sem.at[0]),
        pltpu.make_async_copy(panel_two, l2.at[pl.ds(r * rows2, rows2)], own_sem.at[1]),
        pltpu.make_async_copy(parent, pf.at[pl.ds(r * sub, sub)], own_sem.at[2]),
    ]
    for cp in own:
        cp.start()

    def z_copies(dz):
        dev = to_row(((zi + dz) % nz) * ny + yi)
        i = dz - 1
        return [
            rcopy(panel_one, l1.at[pl.ds(r * rows1, rows1)], g_send.at[i, 0], g_recv.at[i, 0], dev),
            rcopy(panel_two, l2.at[pl.ds(r * rows2, rows2)], g_send.at[i, 1], g_recv.at[i, 1], dev),
            rcopy(parent, pf.at[pl.ds(r * sub, sub)], g_send.at[i, 2], g_recv.at[i, 2], dev),
        ]

    for dz in range(1, nz):
        for cp in z_copies(dz):
            cp.start()

    def a_copy(k):
        d = (r + k + 1) % nr
        return rcopy(top.at[:, d], arows.at[pl.ds(r * nbr, nbr)], a_send.at[k], a_recv.at[k], to_row(d))

    each(nr - 1, lambda k: a_copy(k).start())
    own_a = pltpu.make_async_copy(top.at[:, r], arows.at[pl.ds(r * nbr, nbr)], own_sem.at[3])
    own_a.start()

    for cp in own:
        cp.wait()

    def y_copies(dz, dy):
        s = ((zi - dz + nz) % nz) * ny + yi
        dev = to_row(zi * ny + (yi + dy) % ny)
        i = dz * (ny - 1) + dy - 1
        a = l1.at[pl.ds(s * rows1, rows1)]
        b = l2.at[pl.ds(s * rows2, rows2)]
        p = pf.at[pl.ds(s * sub, sub)]
        return [
            rcopy(a, a, h_send.at[i, 0], h_recv.at[i, 0], dev),
            rcopy(b, b, h_send.at[i, 1], h_recv.at[i, 1], dev),
            rcopy(p, p, h_send.at[i, 2], h_recv.at[i, 2], dev),
        ]

    for dz in range(nz):
        if dz > 0:
            for cp in z_copies(dz):
                cp.wait_recv()
        for dy in range(1, ny):
            for cp in y_copies(dz, dy):
                cp.start()

    own_a.wait()
    each(nr - 1, lambda k: a_copy(k).wait_recv())

    def b_copy(k):
        d = (c + k + 1) % nc
        return rcopy(arows.at[:, d], zs.at[c], b_send.at[k], b_recv.at[k], to_col(d))

    each(nc - 1, lambda k: b_copy(k).start())
    own_b = pltpu.make_async_copy(arows.at[:, c], zs.at[c], own_sem.at[4])
    own_b.start()
    own_b.wait()
    each(nc - 1, lambda k: b_copy(k).wait_recv())

    nbc = arows.shape[2]

    def pack(j):
        places = [sets_one[j, s] for s in range(S1)]
        cols = [(lax.div(q, nbc), lax.rem(q, nbc)) for q in places]
        for a in range(S1):
            for b in range(S1):
                i = (a * S1 + b) * H
                packed[j, i : i + H, :] = zs[cols[b][0], places[a], cols[b][1]]

    def c_copy(k):
        d = (c + k + 1) % nc
        return rcopy(packed.at[d], landed.at[pl.ds(c * npc, npc)], c_send.at[k], c_recv.at[k], to_col(d))

    def pack_send(k):
        pack((c + k + 1) % nc)
        c_copy(k).start()

    each(nc - 1, pack_send)
    pack(c)
    own_c = pltpu.make_async_copy(packed.at[c], landed.at[pl.ds(c * npc, npc)], own_sem.at[5])
    own_c.start()
    own_c.wait()
    each(nc - 1, lambda k: c_copy(k).wait_recv())

    def assemble(b):
        for a in range(S1):
            for h in range(H):
                i = (a * S1 + b) * H + h
                grid[b, a * sub : (a + 1) * sub, h * LN : (h + 1) * LN] = landed[pl.ds(i, nc, stride=npc), :]

    each(S1, assemble)

    for dz in range(nz):
        for dy in range(1, ny):
            for cp in y_copies(dz, dy):
                cp.wait_recv()

    acc1[...] = jnp.zeros_like(acc1)

    def step_one(b):
        acc1[...] -= mm(grid[b], l1[pl.ds(pl.multiple_of(b * B, B), B), :]).reshape(acc1.shape)

    each(S1, step_one)

    def o1_copy(a):
        g = a * nr + r
        return g // S1, rcopy(
            acc1.at[a], out1.at[pl.ds((g % S1) * sub, sub)],
            o1_send.at[a], o1_recv.at[g % S1], to_row(g // S1),
        )

    def o2_copy(t):
        g = t * nr + r
        return g // S2, rcopy(
            b2s.at[t], out2.at[pl.ds((g % S2) * sub, sub)],
            o2_send.at[t], o2_recv.at[g % S2], to_row(g // S2),
        )

    def send_out(n, copy, src, dst):
        def go(a):
            d, cp = copy(a)

            @pl.when(d != r)
            def _():
                cp.start()

            @pl.when(d == r)
            def _():
                at = ((a * nr + r) % n) * sub
                dst[pl.ds(pl.multiple_of(at, sub), sub), :] = src[a]

        each(n, go)

    def done_out(n, copy, src, dst, send, recv):
        def go(a):
            d, cp = copy(a)

            @pl.when(d != r)
            def _():
                cp.wait_send()

            s = (r * n + a) % nr

            @pl.when(s != r)
            def _():
                rcopy(src.at[0], dst.at[pl.ds(a * sub, sub)], send.at[a], recv.at[a], to_row(s)).wait_recv()

        each(n, go)

    send_out(S1, o1_copy, acc1, out1)

    for a in range(S1):
        low1[a * sub : (a + 1) * sub, :] = l1[pl.ds(pl.multiple_of(a * B + r * sub, sub), sub), :]
    for t in range(S2):
        low2[t * sub : (t + 1) * sub, :] = l2[pl.ds(pl.multiple_of(t * B + r * sub, sub), sub), :]

    square = mm_t(low1[...], acc1[...].reshape(S1 * sub, B))
    part[:, :, 0:B] = square.reshape(nr, sub, B)

    for ch in range(2):
        cs = slice(ch * B, (ch + 1) * B)
        pos = []
        for t in range(S2):
            want = sets_two[2 * c + ch, t]
            at = 0
            for s in range(S1):
                at = at + s * (1 - lax.min(lax.abs(sets_one[c, s] - want), 1))
            pos.append(lax.min(at, S1 - 1))
        acc2[...] = jnp.zeros_like(acc2)
        for t in range(S2):
            acc2[...] += mm(grid[pos[t]], l2[t * B : (t + 1) * B, cs]).reshape(acc2.shape)
        for t in range(S2):
            dir2[t * sub : (t + 1) * sub, :] = acc2[pos[t]]
            upper[t * sub : (t + 1) * sub, :] = acc1[pos[t]]
        pc = pf[:, cs]
        u = upper[...]
        l2c = low2[:, cs]
        b2 = -(dir2[...] + mm(u, pc))
        b2s[:, :, cs] = b2.reshape(S2, sub, B)
        cross = mm_t(u, l2c)
        part[:, :, B + ch * B : 2 * B + ch * B] = cross.reshape(nr, sub, B)
        inner = cross - mm(part[:, :, 0:B].reshape(B, B), pc)
        last = mm_t(pc, inner) - mm_t(l2c, b2) + mm_t(parent[:, cs], mm(pivot_one[...], pc))
        part[:, :, 3 * B + ch * B : 4 * B + ch * B] = last.reshape(nr, sub, B)

    def s_copy(k):
        d = (r + k + 1) % nr
        return rcopy(part.at[d], sums.at[r], s_send.at[k], s_recv.at[k], to_row(d))

    each(nr - 1, lambda k: s_copy(k).start())
    sums[r] = part[r]
    send_out(S2, o2_copy, b2s, out2)
    each(nr - 1, lambda k: s_copy(k).wait_recv())

    total = sums[0]
    for k in range(1, nr):
        total = total + sums[k]
    corner = pivot_one[...] - total[:, 0:B]
    corner_one[...] = corner
    for ch in range(2):
        cs = slice(ch * B, (ch + 1) * B)
        beside[:, cs] = -(mm(corner, pf[:, cs]) + total[:, B + ch * B : 2 * B + ch * B])
        corner_two[:, cs] = pivot_two[:, cs] + total[:, 3 * B + ch * B : 4 * B + ch * B]

    done_out(S1, o1_copy, acc1, out1, o1_send, o1_recv)
    done_out(S2, o2_copy, b2s, out2, o2_send, o2_recv)
    below_one[...] = out1[...]
    below_two[...] = out2[...]

    each(nr - 1, lambda k: a_copy(k).wait_send())
    each(nc - 1, lambda k: b_copy(k).wait_send())
    each(nc - 1, lambda k: c_copy(k).wait_send())
    each(nr - 1, lambda k: s_copy(k).wait_send())
    for dz in range(1, nz):
        for cp in z_copies(dz):
            cp.wait_send()
    for dz in range(nz):
        for dy in range(1, ny):
            for cp in y_copies(dz, dy):
                cp.wait_send()


def on_device(ny, top, panel_one, panel_two, parent, pivot_one, pivot_two, sets_one, sets_two):
    nr = lax.axis_size("prow")
    nc = lax.axis_size("pcol")
    S1 = sets_one.shape[1]
    S2 = sets_two.shape[1]
    B = panel_one.shape[1]
    sub = B // nr
    H = max(B // 128, 1)
    LN = B // H
    NB = top.shape[0] * nr // B
    nbr, nbc = NB // nr, NB // nc
    npc = S1 * S1 * H
    nz = nr // ny
    cfg = (nr, nc, ny, B, S1, S2)
    top = top.reshape(nbr, nr, sub, nbc, H, LN)
    vmem = pl.BlockSpec(memory_space=pltpu.VMEM)
    smem = pl.BlockSpec(memory_space=pltpu.SMEM)
    V = lambda *s: pltpu.VMEM(s, F32)
    D = lambda *s: pltpu.SemaphoreType.DMA(s)
    out = lambda *s: jax.ShapeDtypeStruct(s, F32)
    return pl.pallas_call(
        functools.partial(kernel, cfg),
        out_shape=(
            out(S1 * sub, B), out(sub, B), out(S2 * sub, 2 * B), out(sub, 2 * B), out(sub, 2 * B),
        ),
        in_specs=[smem, smem] + [vmem] * 6,
        out_specs=(vmem,) * 5,
        scratch_shapes=[
            V(NB, sub, nbc, H, LN),
            V(nc, NB, nbc, H, LN),
            V(nc, npc, LN),
            V(nc * npc, LN),
            V(S1, S1 * sub, B),
            V(S1 * B, B),
            V(S2 * B, 2 * B),
            V(B, 2 * B),
            V(S1, sub, B),
            V(S1, sub, B),
            V(S1 * sub, B),
            V(S2 * sub, 2 * B),
            V(S2 * sub, B),
            V(S2 * sub, B),
            V(S2, sub, 2 * B),
            V(nr, sub, 5 * B),
            V(nr, sub, 5 * B),
            V(S1 * sub, B),
            V(S2 * sub, 2 * B),
            D(nr - 1), D(nr - 1), D(nc - 1), D(nc - 1), D(nc - 1), D(nc - 1),
            D(nz - 1, 3), D(nz - 1, 3), D(nz * (ny - 1), 3), D(nz * (ny - 1), 3), D(6),
            D(nr - 1), D(nr - 1), D(S1), D(S1), D(S2), D(S2),
        ],
        compiler_params=pltpu.CompilerParams(
            collective_id=0, has_side_effects=True, vmem_limit_bytes=56 * 1024 * 1024
        ),
    )(sets_one, sets_two, top, panel_one, panel_two, parent, pivot_one, pivot_two)


def solution(mesh):
    spec = P("prow", "pcol")
    return jax.shard_map(
        functools.partial(on_device, 4),
        mesh=mesh,
        in_specs=(spec,) * 6 + (P(), P()),
        out_specs=(spec,) * 5,
        check_vma=False,
    )
```

```python
import functools

import jax
import jax.numpy as jnp
from jax import lax
from jax.experimental import pallas as pl
from jax.experimental.pallas import tpu as pltpu
from jax.sharding import PartitionSpec as P

MESH = pl.DeviceIdType.MESH
EXACT = lax.Precision.HIGHEST
F32 = jnp.float32
DIMS = (4, 4, 4, 2, 2)


def mm(a, b):
    return jnp.dot(a, b, precision=EXACT, preferred_element_type=F32)


def mm_t(a, b):
    return lax.dot_general(
        a, b, (((0,), (0,)), ((), ())), precision=EXACT, preferred_element_type=F32
    )


def kernel(
    cfg,
    sets_one, sets_two, top, panel_one, panel_two, parent, pivot_one, pivot_two,
    below_one, corner_one, below_two, beside, corner_two,
    arows, zs, packed, landed, grid, bundle, lg, l1, l2, pf,
    acc1, acc2, low1, low2, dir2, upper, b2s, part, sibpart, comb, sums, out1, out2, fin, fin_in, out1_in, out2_in,
    swap_sem, a_send, a_recv, b_send, b_recv, c_send, c_recv,
    ring_send, ring_recv, sib_send, sib_recv, own_sem,
    x_send, x_recv, s_send, s_recv, o1_send, o1_recv, o2_send, o2_recv, back_send, back_recv,
):
    B, S1, S2 = cfg
    nx, ny, nzh, nzl, nk = DIMS
    nz = nzh * nzl
    nr = nz * nk
    nc = nx * ny
    sub = B // nr
    H = max(B // 128, 1)
    LN = B // H
    npc = S1 * S1 * H
    share1 = S1 * sub
    share2 = S2 * sub
    gathered = share1 + 2 * share2 + 2 * sub
    half = gathered // 2
    nq = top.shape[0]
    prow = lax.axis_index("prow")
    pcol = lax.axis_index("pcol")
    zh, y = prow // ny, prow % ny
    zl, x, core = pcol // (nx * nk), (pcol // nk) % nx, pcol % nk
    z = zh * nzl + zl
    me = z * nk + core
    line = x * ny + y

    def device(x, y, z, core):
        return ((z // nzl) * ny + y, (z % nzl) * (nx * nk) + x * nk + core)

    def to_member(m):
        return device(x, y, m // nk, m % nk)

    def to_line(d):
        return device(d // ny, d % ny, z, core)

    def node_of(d):
        dy = d % ny
        return (dy // nk) * (nx * nk) + (d // ny) * nk + dy % nk

    partner = device(x, zl * nk + core, zh * nzl + y // nk, y % nk)
    away = y != zl * nk + core
    sibling = device(x, y, z, 1 - core)

    def each(n, f):
        def body(k, _):
            f(k)
            return 0
        lax.fori_loop(0, n, body, 0)

    def rcopy(src, dst, ss, rs, dev):
        return pltpu.make_async_remote_copy(
            src_ref=src, dst_ref=dst, send_sem=ss, recv_sem=rs, device_id=dev, device_id_type=MESH
        )

    barrier = pltpu.get_barrier_semaphore()

    def greet(dev):
        pl.semaphore_signal(barrier, inc=1, device_id=dev, device_id_type=MESH)

    each(nr - 1, lambda k: greet(to_member((me + k + 1) % nr)))
    each(nc - 1, lambda k: greet(to_line((line + k + 1) % nc)))

    @pl.when(away)
    def _():
        greet(partner)

    bundle[0:share1, :] = panel_one[...]
    at = share1
    for ch in range(2):
        bundle[at : at + share2, :] = panel_two[:, ch * B : (ch + 1) * B]
        at += share2
    for ch in range(2):
        bundle[at : at + sub, :] = parent[:, ch * B : (ch + 1) * B]
        at += sub
    bundle[at : at + sub, :] = pivot_one[...]
    at += sub
    for ch in range(2):
        bundle[at : at + sub, :] = pivot_two[:, ch * B : (ch + 1) * B]
        at += sub

    pl.semaphore_wait(barrier, nr + nc - 2 + lax.min(lax.abs(y - (zl * nk + core)), 1))

    swap = rcopy(bundle, lg.at[prow], swap_sem.at[0], swap_sem.at[1], partner)

    @pl.when(away)
    def _():
        swap.start()

    def a_copy(k):
        d = (me + k + 1) % nr
        return rcopy(top.at[:, d], arows.at[pl.ds(me * nq, nq)], a_send.at[k], a_recv.at[k], to_member(d))

    each(nr - 1, lambda k: a_copy(k).start())
    own_a = pltpu.make_async_copy(top.at[:, me], arows.at[pl.ds(me * nq, nq)], own_sem.at[0])
    own_a.start()

    @pl.when(away)
    def _():
        swap.wait_recv()

    @pl.when(jnp.logical_not(away))
    def _():
        lg[prow] = bundle[...]

    steps = nz // 2

    def ring_copy(way, s):
        to = (z + way + nz) % nz
        owner = ((z - way * s + nz) % nz) * nk + core
        w = 0 if way == 1 else 1
        if s < steps - 1:
            rows = pl.ds(0, gathered)
        else:
            rows = pl.ds(w * half, half)
        ref = lg.at[owner, rows]
        return rcopy(ref, ref, ring_send.at[w, s], ring_recv.at[w, s], device(x, y, to, core))

    def sib_copy(way, s):
        w = 0 if way == 1 else 1
        owner = ((z - way * s + nz) % nz) * nk + core
        if s < steps:
            rows = pl.ds(0, gathered)
        else:
            rows = pl.ds(w * half, half)
        ref = lg.at[owner, rows]
        i = 0 if s == 0 else 1 + w * steps + s - 1
        return rcopy(ref, ref, sib_send.at[i], sib_recv.at[i], sibling)

    WAYS = (1, -1)

    def pass_on(s):
        for way in WAYS:
            ring_copy(way, s - 1).wait_recv()
            if s < steps:
                ring_copy(way, s).start()
            sib_copy(way, s).start()

    for way in WAYS:
        ring_copy(way, 0).start()
    sib_copy(1, 0).start()

    own_a.wait()
    each(nr - 1, lambda k: a_copy(k).wait_recv())

    nb = nr * nq

    def b_copy(k):
        d = (line + k + 1) % nc
        return rcopy(arows.at[:, d], zs.at[pl.ds(line * nb, nb)], b_send.at[k], b_recv.at[k], to_line(d))

    each(nc - 1, lambda k: b_copy(k).start())
    own_b = pltpu.make_async_copy(arows.at[:, line], zs.at[pl.ds(line * nb, nb)], own_sem.at[1])
    own_b.start()

    pass_on(1)

    own_b.wait()
    each(nc - 1, lambda k: b_copy(k).wait_recv())

    nbr = 2
    nbc = nq // nbr

    def pack(d):
        j = node_of(d)
        rows, cols = [], []
        for s in range(S1):
            q = sets_one[j, s]
            r = lax.div(q, nbr)
            rows.append(lax.rem(r, ny) * nb + lax.div(r, ny) * (nzl * nk * nq) + lax.rem(q, nbr) * nbc)
            c = lax.div(q, nbc)
            cc = lax.div(c, nk)
            cols.append(
                lax.rem(cc, nx) * (ny * nb) + lax.div(cc, nx) * (nk * nq) + lax.rem(c, nk) * nq + lax.rem(q, nbc)
            )
        for a in range(S1):
            for b in range(S1):
                i = (a * S1 + b) * H
                packed[d, i : i + H, :] = zs[rows[a] + cols[b]]

    def c_copy(k):
        d = (line + k + 1) % nc
        return rcopy(packed.at[d], landed.at[pl.ds(line * npc, npc)], c_send.at[k], c_recv.at[k], to_line(d))

    def pack_send(k):
        pack((line + k + 1) % nc)
        c_copy(k).start()

    each(nc - 1, pack_send)
    pack(line)
    own_c = pltpu.make_async_copy(packed.at[line], landed.at[pl.ds(line * npc, npc)], own_sem.at[2])
    own_c.start()

    for s in range(2, steps + 1):
        pass_on(s)

    sib_copy(1, 0).wait_recv()
    for s in range(1, steps + 1):
        for way in WAYS:
            sib_copy(way, s).wait_recv()

    def spread(m):
        l1[pl.ds(m * share1, share1), :] = lg[m, 0:share1, :]
        for ch in range(2):
            o = share1 + ch * share2
            l2[ch, pl.ds(m * share2, share2), :] = lg[m, o : o + share2, :]
            o = share1 + 2 * share2 + ch * sub
            pf[ch, pl.ds(m * sub, sub), :] = lg[m, o : o + sub, :]

    each(nr, spread)

    own_c.wait()
    each(nc - 1, lambda k: c_copy(k).wait_recv())

    def assemble(b):
        for a in range(S1):
            for h in range(H):
                i = (a * S1 + b) * H + h
                grid[b, a * sub : (a + 1) * sub, h * LN : (h + 1) * LN] = landed[pl.ds(i, nc, stride=npc), :]

    each(S1, assemble)

    acc1[...] = jnp.zeros_like(acc1)

    def step_one(b):
        acc1[...] -= mm(grid[b], l1[pl.ds(pl.multiple_of(b * B, B), B), :]).reshape(acc1.shape)

    each(S1, step_one)

    def o1_copy(a):
        g = a * nr + me
        return g // S1, rcopy(
            acc1.at[a], out1.at[pl.ds((g % S1) * sub, sub)],
            o1_send.at[a], o1_recv.at[g % S1], to_member(g // S1),
        )

    def o2_copy(t):
        g = t * nr + me
        return g // S2, rcopy(
            b2s.at[t], out2.at[pl.ds((g % S2) * sub, sub)],
            o2_send.at[t], o2_recv.at[g % S2], to_member(g // S2),
        )

    def send_out(n, copy, src, dst):
        def go(a):
            d, cp = copy(a)

            @pl.when(d != me)
            def _():
                cp.start()

            @pl.when(d == me)
            def _():
                at = ((a * nr + me) % n) * sub
                dst[pl.ds(pl.multiple_of(at, sub), sub), :] = src[a]

        each(n, go)

    def take_out(n, src, dst, send, recv):
        def go(a):
            s = (me * n + a) % nr

            @pl.when(s != me)
            def _():
                rcopy(src.at[0], dst.at[pl.ds(a * sub, sub)], send.at[a], recv.at[a], to_member(s)).wait_recv()

        each(n, go)

    def done_out(n, copy):
        def go(a):
            d, cp = copy(a)

            @pl.when(d != me)
            def _():
                cp.wait_send()

        each(n, go)

    send_out(S1, o1_copy, acc1, out1)

    def x_copy(g, cs):
        return rcopy(part.at[:, 1 - core, :, cs], sibpart.at[:, :, cs], x_send.at[g], x_recv.at[g], sibling)

    def s_copy(g, cs, k):
        d = (z + k + 1) % nz
        return rcopy(comb.at[d, :, cs], sums.at[z, :, cs], s_send.at[g, k], s_recv.at[g, k], device(x, y, d, core))

    spans = [pl.ds(0, B), pl.ds(B, 2 * B), pl.ds(3 * B, 2 * B)]

    def combine(g):
        cs = spans[g]
        x_copy(g, cs).wait_recv()
        comb[:, :, cs] = part[:, core, :, cs] + sibpart[:, :, cs]
        for k in range(nz - 1):
            s_copy(g, cs, k).start()

    node = node_of(line)
    for a in range(S1):
        low1[a * sub : (a + 1) * sub, :] = l1[pl.ds(pl.multiple_of(a * B + me * sub, sub), sub), :]
    square = mm_t(low1[...], acc1[...].reshape(S1 * sub, B))
    part[:, :, :, 0:B] = square.reshape(nz, nk, sub, B)
    x_copy(0, spans[0]).start()
    pivot1 = lg[me, gathered : gathered + sub, :]

    for ch in range(2):
        for t in range(S2):
            low2[t * sub : (t + 1) * sub, :] = l2[ch, pl.ds(pl.multiple_of(t * B + me * sub, sub), sub), :]
        pos = []
        for t in range(S2):
            want = sets_two[2 * node + ch, t]
            at = 0
            for s in range(S1):
                at = at + s * (1 - lax.min(lax.abs(sets_one[node, s] - want), 1))
            pos.append(lax.min(at, S1 - 1))
        acc2[...] = jnp.zeros_like(acc2)
        for t in range(S2):
            acc2[...] += mm(grid[pos[t]], l2[ch, t * B : (t + 1) * B, :]).reshape(acc2.shape)
        for t in range(S2):
            dir2[t * sub : (t + 1) * sub, :] = acc2[pos[t]]
            upper[t * sub : (t + 1) * sub, :] = acc1[pos[t]]
        pc = pf[ch]
        u = upper[...]
        l2c = low2[...]
        b2 = -(dir2[...] + mm(u, pc))
        b2s[:, :, ch * B : (ch + 1) * B] = b2.reshape(S2, sub, B)
        cross = mm_t(u, l2c)
        inner = cross - mm(part[:, :, :, 0:B].reshape(B, B), pc)
        mine = pf[ch, pl.ds(pl.multiple_of(me * sub, sub), sub), :]
        last = mm_t(pc, inner) - mm_t(l2c, b2) + mm_t(mine, mm(pivot1, pc))
        o = B + 2 * ch * B
        part[:, :, :, o : o + B] = cross.reshape(nz, nk, sub, B)
        part[:, :, :, o + B : o + 2 * B] = last.reshape(nz, nk, sub, B)
        x_copy(ch + 1, spans[ch + 1]).start()
        combine(ch)

    send_out(S2, o2_copy, b2s, out2)
    combine(2)

    take_out(S1, acc1, out1, o1_send, o1_recv)
    take_out(S2, b2s, out2, o2_send, o2_recv)
    backs = [
        rcopy(out1, out1_in, back_send.at[0], back_recv.at[0], partner),
        rcopy(out2, out2_in, back_send.at[1], back_recv.at[1], partner),
        rcopy(fin, fin_in, back_send.at[2], back_recv.at[2], partner),
    ]

    @pl.when(away)
    def _():
        backs[0].start()
        backs[1].start()

    for g in range(3):
        for k in range(nz - 1):
            s_copy(g, spans[g], k).wait_recv()

    total = comb[z]
    for k in range(1, nz):
        total = total + sums[(z + k) % nz]
    corner = pivot1 - total[:, 0:B]
    fin[:, 0:B] = corner
    for ch in range(2):
        o = B + 2 * ch * B
        p2 = gathered + sub + ch * sub
        fin[:, (1 + ch) * B : (2 + ch) * B] = -(mm(corner, pf[ch]) + total[:, o : o + B])
        fin[:, (3 + ch) * B : (4 + ch) * B] = lg[me, p2 : p2 + sub, :] + total[:, o + B : o + 2 * B]

    def deliver(o1, o2, f):
        below_one[...] = o1[...]
        below_two[...] = o2[...]
        corner_one[...] = f[:, 0:B]
        beside[...] = f[:, B : 3 * B]
        corner_two[...] = f[:, 3 * B : 5 * B]

    @pl.when(away)
    def _():
        backs[2].start()
        for cp in backs:
            cp.wait_recv()
        deliver(out1_in, out2_in, fin_in)

    @pl.when(jnp.logical_not(away))
    def _():
        deliver(out1, out2, fin)

    @pl.when(away)
    def _():
        swap.wait_send()
        for cp in backs:
            cp.wait_send()

    each(nr - 1, lambda k: a_copy(k).wait_send())
    each(nc - 1, lambda k: b_copy(k).wait_send())
    each(nc - 1, lambda k: c_copy(k).wait_send())
    for way in WAYS:
        for s in range(steps):
            ring_copy(way, s).wait_send()
            sib_copy(way, s + 1).wait_send()
    sib_copy(1, 0).wait_send()
    for g in range(3):
        x_copy(g, spans[g]).wait_send()
        for k in range(nz - 1):
            s_copy(g, spans[g], k).wait_send()
    done_out(S1, o1_copy)
    done_out(S2, o2_copy)


def on_device(top, panel_one, panel_two, parent, pivot_one, pivot_two, sets_one, sets_two):
    nx, ny, nzh, nzl, nk = DIMS
    nz = nzh * nzl
    nr = nz * nk
    nc = nx * ny
    S1 = sets_one.shape[1]
    S2 = sets_two.shape[1]
    B = panel_one.shape[1]
    sub = B // nr
    H = max(B // 128, 1)
    LN = B // H
    nbr, nbc = top.shape[0] // B, top.shape[1] // B
    nq = nbr * nbc
    npc = S1 * S1 * H
    share1, share2 = S1 * sub, S2 * sub
    gathered = share1 + 2 * share2 + 2 * sub
    whole = gathered + 3 * sub
    steps = nz // 2
    cfg = (B, S1, S2)
    top = top.reshape(nbr, nr, sub, nbc, H, LN).transpose(0, 3, 1, 2, 4, 5).reshape(nq, nr, sub, H, LN)
    vmem = pl.BlockSpec(memory_space=pltpu.VMEM)
    smem = pl.BlockSpec(memory_space=pltpu.SMEM)
    V = lambda *s: pltpu.VMEM(s, F32)
    D = lambda *s: pltpu.SemaphoreType.DMA(s)
    out = lambda *s: jax.ShapeDtypeStruct(s, F32)
    return pl.pallas_call(
        functools.partial(kernel, cfg),
        out_shape=(
            out(share1, B), out(sub, B), out(share2, 2 * B), out(sub, 2 * B), out(sub, 2 * B),
        ),
        in_specs=[smem, smem] + [vmem] * 6,
        out_specs=(vmem,) * 5,
        scratch_shapes=[
            V(nr * nq, sub, H, LN),
            V(nc * nr * nq, H, LN),
            V(nc, npc, LN),
            V(nc * npc, LN),
            V(S1, share1, B),
            V(whole, B),
            V(nr, whole, B),
            V(S1 * B, B),
            V(2, S2 * B, B),
            V(2, B, B),
            V(S1, sub, B),
            V(S1, sub, B),
            V(share1, B),
            V(share2, B),
            V(share2, B),
            V(share2, B),
            V(S2, sub, 2 * B),
            V(nz, nk, sub, 5 * B),
            V(nz, sub, 5 * B),
            V(nz, sub, 5 * B),
            V(nz, sub, 5 * B),
            V(share1, B),
            V(share2, 2 * B),
            V(sub, 5 * B),
            V(sub, 5 * B),
            V(share1, B),
            V(share2, 2 * B),
            D(2),
            D(nr - 1), D(nr - 1), D(nc - 1), D(nc - 1), D(nc - 1), D(nc - 1),
            D(2, steps), D(2, steps), D(1 + 2 * steps), D(1 + 2 * steps), D(3),
            D(3), D(3), D(3, nz - 1), D(3, nz - 1), D(S1), D(S1), D(S2), D(S2), D(3), D(3),
        ],
        compiler_params=pltpu.CompilerParams(
            collective_id=0, has_side_effects=True, vmem_limit_bytes=56 * 1024 * 1024
        ),
    )(sets_one, sets_two, top, panel_one, panel_two, parent, pivot_one, pivot_two)


def solution(mesh):
    spec = P("prow", "pcol")
    return jax.shard_map(
        on_device,
        mesh=mesh,
        in_specs=(spec,) * 6 + (P(), P()),
        out_specs=(spec,) * 5,
        check_vma=False,
    )
```

```python
import functools

import jax
import jax.numpy as jnp
from jax import lax
from jax.experimental import pallas as pl
from jax.experimental.pallas import tpu as pltpu
from jax.sharding import PartitionSpec as P

MESH = pl.DeviceIdType.MESH
EXACT = lax.Precision.HIGHEST
F32 = jnp.float32
DIMS = (4, 4, 4, 2, 2)


def mm(a, b):
    return jnp.dot(a, b, precision=EXACT, preferred_element_type=F32)


def mm_t(a, b):
    return lax.dot_general(
        a, b, (((0,), (0,)), ((), ())), precision=EXACT, preferred_element_type=F32
    )


def kernel(
    cfg,
    sets_one, sets_two, top, panel_one, panel_two, parent, pivot_one, pivot_two,
    out1_in, out2_in, fin_in,
    arows, zs, packed, landed, grid, bundle, lg, l1, l2, pf,
    acc1, acc2, low1, low2, dir2, upper, b2s, part, sibpart, comb, sums, out1, out2, fin,
    swap_sem, a_send, a_recv, b_send, b_recv, c_send, c_recv,
    ring_send, ring_recv, sib_send, sib_recv, own_sem,
    x_send, x_recv, s_send, s_recv, o1_send, o1_recv, o2_send, o2_recv, back_send, back_recv,
):
    B, S1, S2 = cfg
    nx, ny, nzh, nzl, nk = DIMS
    nz = nzh * nzl
    nr = nz * nk
    nc = nx * ny
    sub = B // nr
    H = max(B // 128, 1)
    LN = B // H
    npc = S1 * S1 * H
    share1 = S1 * sub
    share2 = S2 * sub
    gathered = share1 + 2 * share2 + 2 * sub
    half = gathered // 2
    nq = top.shape[0]
    prow = lax.axis_index("prow")
    pcol = lax.axis_index("pcol")
    div, rem = lax.div, lax.rem
    zh, y = div(prow, ny), rem(prow, ny)
    zl, x, core = div(pcol, nx * nk), rem(div(pcol, nk), nx), rem(pcol, nk)
    z = zh * nzl + zl
    line = x * ny + y
    spot = z * nk + core
    y_hi, y_lo = div(y, nk), rem(y, nk)
    turn = y_lo if nzl == 2 else y_lo * 0

    def flip(a, b):
        return a + b - 2 * a * b

    def virtual(zz):
        return zz + turn * (1 - 2 * rem(zz, 2)) if nzl == 2 else zz

    zeta = virtual(z)
    me = zeta * nk + core

    def device(x, y, z, core):
        return (div(z, nzl) * ny + y, rem(z, nzl) * (nx * nk) + x * nk + core)

    def to_member(m):
        return device(x, y, virtual(div(m, nk)), rem(m, nk))

    def to_spot(m):
        return device(x, y, div(m, nk), rem(m, nk))

    def share_of(zz, k):
        return virtual(zz) * nk + k

    def node_of(dx, dy):
        return div(dy, nk) * (nx * nk) + dx * nk + rem(dy, nk)

    taker = device(x, zl * nk + core, zh * nzl + (flip(y_hi, core) if nzl == 2 else y_hi), y_lo)
    holder = device(x, (flip(zl, y_lo) if nzl == 2 else zl) * nk + core, zh * nzl + y_hi, y_lo)
    apart = lax.min(lax.abs(y - (zl * nk + core)) + (core if nzl == 2 else core * 0), 1)
    away = apart == 1
    sibling = device(x, y, z, 1 - core)

    if nx == 4 and ny == 4:
        near = [(1, 0), (3, 0), (0, 1), (0, 3), (1, 1), (3, 3), (1, 3), (3, 1),
                (2, 0), (0, 2), (2, 1), (2, 3), (1, 2), (3, 2), (2, 2)]
    else:
        near = [(i, j) for i in range(nx) for j in range(ny) if i + j > 0]

    def shift(k):
        dx = near[k][0] + core * (near[nc - 2 - k][0] - near[k][0])
        dy = near[k][1] + core * (near[nc - 2 - k][1] - near[k][1])
        return rem(x + dx, nx), rem(y + dy, ny), dx * ny + dy

    def each(n, f):
        def body(k, _):
            f(k)
            return 0
        lax.fori_loop(0, n, body, 0)

    def rcopy(src, dst, ss, rs, dev):
        return pltpu.make_async_remote_copy(
            src_ref=src, dst_ref=dst, send_sem=ss, recv_sem=rs, device_id=dev, device_id_type=MESH
        )

    barrier = pltpu.get_barrier_semaphore()

    def greet(dev):
        pl.semaphore_signal(barrier, inc=1, device_id=dev, device_id_type=MESH)

    for dz in range(nz):
        for dk in range(nk):
            if dz + dk > 0:
                greet(device(x, y, rem(z + dz, nz), rem(core + dk, nk)))
    for dx, dy in near:
        greet(device(rem(x + dx, nx), rem(y + dy, ny), z, core))

    @pl.when(away)
    def _():
        greet(taker)
        greet(holder)

    bundle[0:share1, :] = panel_one[...]
    at = share1
    for ch in range(2):
        bundle[at : at + share2, :] = panel_two[:, ch * B : (ch + 1) * B]
        at += share2
    for ch in range(2):
        bundle[at : at + sub, :] = parent[:, ch * B : (ch + 1) * B]
        at += sub
    bundle[at : at + sub, :] = pivot_one[...]
    at += sub
    for ch in range(2):
        bundle[at : at + sub, :] = pivot_two[:, ch * B : (ch + 1) * B]
        at += sub

    pl.semaphore_wait(barrier, nr + nc - 2 + 2 * apart)

    swap = rcopy(bundle, lg.at[prow], swap_sem.at[0], swap_sem.at[1], taker)

    @pl.when(away)
    def _():
        swap.start()

    def a_copy(k):
        d = rem(spot + k + 1, nr)
        return rcopy(top.at[:, d], arows.at[pl.ds(spot * nq, nq)], a_send.at[k], a_recv.at[k], to_spot(d))

    each(nr - 1, lambda k: a_copy(k).start())
    own_a = pltpu.make_async_copy(top.at[:, spot], arows.at[pl.ds(spot * nq, nq)], own_sem.at[0])
    own_a.start()

    steps = nz // 2
    STREAMS = [(1, 0), (-1, 1), (1, 1), (-1, 0)]

    def length(way, piece):
        return steps if (way == 1) == (piece == 0) else steps - 1

    def ring_copy(way, piece, s):
        to = rem(z + way + nz, nz)
        owner = share_of(rem(z - way * s + nz, nz), core)
        ref = lg.at[owner, pl.ds(piece * half, half)]
        w = 0 if way == 1 else 1
        return rcopy(ref, ref, ring_send.at[w, piece, s], ring_recv.at[w, piece, s], device(x, y, to, core))

    def sib_copy(way, piece, s):
        owner = share_of(rem(z - way * s + nz, nz), core)
        ref = lg.at[owner, pl.ds(piece * half, half)]
        w = 0 if way == 1 else 1
        return rcopy(ref, ref, sib_send.at[w, piece, s], sib_recv.at[w, piece, s], sibling)

    def pass_on(s):
        for way, piece in STREAMS:
            n = length(way, piece)
            if s <= n:
                ring_copy(way, piece, s - 1).wait_recv()
                if s < n:
                    ring_copy(way, piece, s).start()
                sib_copy(way, piece, s).start()

    own_a.wait()
    each(nr - 1, lambda k: a_copy(k).wait_recv())

    nb = nr * nq

    def b_copy(k):
        dx, dy, n = shift(k)
        return rcopy(
            arows.at[:, dx * ny + dy], zs.at[pl.ds(line * nb, nb)], b_send.at[n], b_recv.at[n], device(dx, dy, z, core)
        )

    for k in range(nc - 1):
        b_copy(k).start()
    own_b = pltpu.make_async_copy(arows.at[:, line], zs.at[pl.ds(line * nb, nb)], own_sem.at[1])
    own_b.start()

    @pl.when(away)
    def _():
        swap.wait_recv()

    @pl.when(jnp.logical_not(away))
    def _():
        lg[prow] = bundle[...]

    for way, piece in STREAMS:
        if length(way, piece) > 0:
            ring_copy(way, piece, 0).start()
    for piece in range(2):
        sib_copy(1, piece, 0).start()

    pass_on(1)

    own_b.wait()
    for k in range(nc - 1):
        b_copy(k).wait_recv()

    nbr = 2
    nbc = nq // nbr

    def pack(dx, dy):
        d = dx * ny + dy
        j = node_of(dx, dy)
        cols = []
        for s in range(S1):
            q = sets_one[j, s]
            c = div(q, nbc)
            cc = div(c, nk)
            cols.append(rem(cc, nx) * (ny * nb) + div(cc, nx) * (nk * nq) + rem(c, nk) * nq + rem(q, nbc))

        def row(a):
            p = sets_one[j, a]
            r = div(p, nbr)
            at = rem(r, ny) * nb + div(r, ny) * (nzl * nk * nq) + rem(p, nbr) * nbc
            for b in range(S1):
                packed[d, pl.ds((a * S1 + b) * H, H), :] = zs[at + cols[b]]

        each(S1, row)

    def c_copy(k):
        dx, dy, n = shift(k)
        return rcopy(
            packed.at[dx * ny + dy], landed.at[pl.ds(line * npc, npc)], c_send.at[n], c_recv.at[n],
            device(dx, dy, z, core),
        )

    for k in range(nc - 1):
        pack(*shift(k)[:2])
        c_copy(k).start()
    pack(x, y)
    own_c = pltpu.make_async_copy(packed.at[line], landed.at[pl.ds(line * npc, npc)], own_sem.at[2])
    own_c.start()

    for s in range(2, steps + 1):
        pass_on(s)

    for piece in range(2):
        sib_copy(1, piece, 0).wait_recv()
    for s in range(1, steps + 1):
        for way, piece in STREAMS:
            if s <= length(way, piece):
                sib_copy(way, piece, s).wait_recv()

    def spread(m):
        l1[pl.ds(m * share1, share1), :] = lg[m, 0:share1, :]
        for ch in range(2):
            o = share1 + ch * share2
            l2[ch, pl.ds(m * share2, share2), :] = lg[m, o : o + share2, :]
            o = share1 + 2 * share2 + ch * sub
            pf[ch, pl.ds(m * sub, sub), :] = lg[m, o : o + sub, :]

    each(nr, spread)

    own_c.wait()
    for k in range(nc - 1):
        c_copy(k).wait_recv()

    def assemble(b):
        for a in range(S1):
            for h in range(H):
                i = (a * S1 + b) * H + h
                grid[b, a * sub : (a + 1) * sub, h * LN : (h + 1) * LN] = landed[pl.ds(i, nc, stride=npc), :]

    each(S1, assemble)

    acc1[...] = jnp.zeros_like(acc1)

    def step_one(b):
        acc1[...] -= mm(grid[b], l1[pl.ds(pl.multiple_of(b * B, B), B), :]).reshape(acc1.shape)

    each(S1, step_one)

    def o1_copy(a):
        g = a * nr + spot
        return div(g, S1), rcopy(
            acc1.at[a], out1.at[pl.ds((rem(g, S1)) * sub, sub)],
            o1_send.at[a], o1_recv.at[rem(g, S1)], to_member(div(g, S1)),
        )

    def o2_copy(t):
        g = t * nr + spot
        return div(g, S2), rcopy(
            b2s.at[t], out2.at[pl.ds((rem(g, S2)) * sub, sub)],
            o2_send.at[t], o2_recv.at[rem(g, S2)], to_member(div(g, S2)),
        )

    def send_out(n, copy, src, dst):
        def go(a):
            d, cp = copy(a)

            @pl.when(d != me)
            def _():
                cp.start()

            @pl.when(d == me)
            def _():
                at = rem(a * nr + spot, n) * sub
                dst[pl.ds(pl.multiple_of(at, sub), sub), :] = src[a]

        each(n, go)

    def take_out(n, src, dst, send, recv):
        def go(a):
            s = rem(me * n + a, nr)

            @pl.when(s != spot)
            def _():
                rcopy(src.at[0], dst.at[pl.ds(a * sub, sub)], send.at[a], recv.at[a], to_spot(s)).wait_recv()

        each(n, go)

    def done_out(n, copy):
        def go(a):
            d, cp = copy(a)

            @pl.when(d != me)
            def _():
                cp.wait_send()

        each(n, go)

    send_out(S1, o1_copy, acc1, out1)

    def x_copy(g, cs):
        return rcopy(part.at[:, 1 - core, :, cs], sibpart.at[:, :, cs], x_send.at[g], x_recv.at[g], sibling)

    def s_copy(g, cs, k):
        d = rem(zeta + k + 1, nz)
        return rcopy(
            comb.at[d, :, cs], sums.at[zeta, :, cs], s_send.at[g, k], s_recv.at[g, k], device(x, y, virtual(d), core)
        )

    spans = [pl.ds(0, B), pl.ds(B, 2 * B), pl.ds(3 * B, 2 * B)]

    def combine(g):
        cs = spans[g]
        x_copy(g, cs).wait_recv()
        comb[:, :, cs] = part[:, core, :, cs] + sibpart[:, :, cs]
        for k in range(nz - 1):
            s_copy(g, cs, k).start()

    node = node_of(x, y)
    for a in range(S1):
        low1[a * sub : (a + 1) * sub, :] = l1[pl.ds(pl.multiple_of(a * B + spot * sub, sub), sub), :]
    square = mm_t(low1[...], acc1[...].reshape(S1 * sub, B))
    part[:, :, :, 0:B] = square.reshape(nz, nk, sub, B)
    x_copy(0, spans[0]).start()
    pivot1 = lg[me, gathered : gathered + sub, :]

    for ch in range(2):
        for t in range(S2):
            low2[t * sub : (t + 1) * sub, :] = l2[ch, pl.ds(pl.multiple_of(t * B + spot * sub, sub), sub), :]
        pos = []
        for t in range(S2):
            want = sets_two[2 * node + ch, t]
            at = 0
            for s in range(S1):
                at = at + s * (1 - lax.min(lax.abs(sets_one[node, s] - want), 1))
            pos.append(lax.min(at, S1 - 1))
        acc2[...] = jnp.zeros_like(acc2)
        for t in range(S2):
            acc2[...] += mm(grid[pos[t]], l2[ch, t * B : (t + 1) * B, :]).reshape(acc2.shape)
        for t in range(S2):
            dir2[t * sub : (t + 1) * sub, :] = acc2[pos[t]]
            upper[t * sub : (t + 1) * sub, :] = acc1[pos[t]]
        pc = pf[ch]
        u = upper[...]
        l2c = low2[...]
        b2 = -(dir2[...] + mm(u, pc))
        b2s[:, :, ch * B : (ch + 1) * B] = b2.reshape(S2, sub, B)
        cross = mm_t(u, l2c)
        inner = cross - mm(part[:, :, :, 0:B].reshape(B, B), pc)
        mine = pf[ch, pl.ds(pl.multiple_of(me * sub, sub), sub), :]
        last = mm_t(pc, inner) - mm_t(l2c, b2) + mm_t(mine, mm(pivot1, pc))
        o = B + 2 * ch * B
        part[:, :, :, o : o + B] = cross.reshape(nz, nk, sub, B)
        part[:, :, :, o + B : o + 2 * B] = last.reshape(nz, nk, sub, B)
        x_copy(ch + 1, spans[ch + 1]).start()
        combine(ch)

    send_out(S2, o2_copy, b2s, out2)
    combine(2)

    take_out(S1, acc1, out1, o1_send, o1_recv)
    take_out(S2, b2s, out2, o2_send, o2_recv)
    backs = [
        rcopy(out1, out1_in, back_send.at[0], back_recv.at[0], holder),
        rcopy(out2, out2_in, back_send.at[1], back_recv.at[1], holder),
        rcopy(fin, fin_in, back_send.at[2], back_recv.at[2], holder),
    ]

    @pl.when(away)
    def _():
        backs[0].start()
        backs[1].start()

    for g in range(3):
        for k in range(nz - 1):
            s_copy(g, spans[g], k).wait_recv()

    total = comb[zeta]
    for k in range(1, nz):
        total = total + sums[rem(zeta + k, nz)]
    corner = pivot1 - total[:, 0:B]
    fin[:, 0:B] = corner
    for ch in range(2):
        o = B + 2 * ch * B
        p2 = gathered + sub + ch * sub
        fin[:, (1 + ch) * B : (2 + ch) * B] = -(mm(corner, pf[ch]) + total[:, o : o + B])
        fin[:, (3 + ch) * B : (4 + ch) * B] = lg[me, p2 : p2 + sub, :] + total[:, o + B : o + 2 * B]

    @pl.when(away)
    def _():
        backs[2].start()
        for cp in backs:
            cp.wait_recv()

    @pl.when(jnp.logical_not(away))
    def _():
        out1_in[...] = out1[...]
        out2_in[...] = out2[...]
        fin_in[...] = fin[...]

    @pl.when(away)
    def _():
        swap.wait_send()
        for cp in backs:
            cp.wait_send()

    each(nr - 1, lambda k: a_copy(k).wait_send())
    for k in range(nc - 1):
        b_copy(k).wait_send()
        c_copy(k).wait_send()
    for way, piece in STREAMS:
        for s in range(length(way, piece)):
            ring_copy(way, piece, s).wait_send()
            sib_copy(way, piece, s + 1).wait_send()
    for piece in range(2):
        sib_copy(1, piece, 0).wait_send()
    for g in range(3):
        x_copy(g, spans[g]).wait_send()
        for k in range(nz - 1):
            s_copy(g, spans[g], k).wait_send()
    done_out(S1, o1_copy)
    done_out(S2, o2_copy)


def deliver(one, two, rest, below_one, corner_one, below_two, beside, corner_two):
    B = one.shape[1]
    below_one[...] = one[...]
    below_two[...] = two[...]
    corner_one[...] = rest[:, 0:B]
    beside[...] = rest[:, B : 3 * B]
    corner_two[...] = rest[:, 3 * B : 5 * B]


def on_device(top, panel_one, panel_two, parent, pivot_one, pivot_two, sets_one, sets_two):
    nx, ny, nzh, nzl, nk = DIMS
    nz = nzh * nzl
    nr = nz * nk
    nc = nx * ny
    S1 = sets_one.shape[1]
    S2 = sets_two.shape[1]
    B = panel_one.shape[1]
    sub = B // nr
    H = max(B // 128, 1)
    LN = B // H
    nbr, nbc = top.shape[0] // B, top.shape[1] // B
    nq = nbr * nbc
    npc = S1 * S1 * H
    share1, share2 = S1 * sub, S2 * sub
    gathered = share1 + 2 * share2 + 2 * sub
    whole = gathered + 3 * sub
    steps = nz // 2
    cfg = (B, S1, S2)
    top = top.reshape(nbr, nr, sub, nbc, H, LN).transpose(0, 3, 1, 2, 4, 5).reshape(nq, nr, sub, H, LN)
    vmem = pl.BlockSpec(memory_space=pltpu.VMEM)
    smem = pl.BlockSpec(memory_space=pltpu.SMEM)
    V = lambda *s: pltpu.VMEM(s, F32)
    D = lambda *s: pltpu.SemaphoreType.DMA(s)
    out = lambda *s: jax.ShapeDtypeStruct(s, F32)
    one, two, rest = pl.pallas_call(
        functools.partial(kernel, cfg),
        out_shape=(out(share1, B), out(share2, 2 * B), out(sub, 5 * B)),
        in_specs=[smem, smem] + [vmem] * 6,
        out_specs=(vmem,) * 3,
        scratch_shapes=[
            V(nr * nq, sub, H, LN),
            V(nc * nr * nq, H, LN),
            V(nc, npc, LN),
            V(nc * npc, LN),
            V(S1, share1, B),
            V(whole, B),
            V(nr, whole, B),
            V(S1 * B, B),
            V(2, S2 * B, B),
            V(2, B, B),
            V(S1, sub, B),
            V(S1, sub, B),
            V(share1, B),
            V(share2, B),
            V(share2, B),
            V(share2, B),
            V(S2, sub, 2 * B),
            V(nz, nk, sub, 5 * B),
            V(nz, sub, 5 * B),
            V(nz, sub, 5 * B),
            V(nz, sub, 5 * B),
            V(share1, B),
            V(share2, 2 * B),
            V(sub, 5 * B),
            D(2),
            D(nr - 1), D(nr - 1), D(nc), D(nc), D(nc), D(nc),
            D(2, 2, steps), D(2, 2, steps), D(2, 2, steps + 1), D(2, 2, steps + 1), D(3),
            D(3), D(3), D(3, nz - 1), D(3, nz - 1), D(S1), D(S1), D(S2), D(S2), D(3), D(3),
        ],
        compiler_params=pltpu.CompilerParams(
            collective_id=0, has_side_effects=True, vmem_limit_bytes=56 * 1024 * 1024
        ),
    )(sets_one, sets_two, top, panel_one, panel_two, parent, pivot_one, pivot_two)
    return pl.pallas_call(
        deliver,
        out_shape=(out(share1, B), out(sub, B), out(share2, 2 * B), out(sub, 2 * B), out(sub, 2 * B)),
        in_specs=[vmem] * 3,
        out_specs=(vmem,) * 5,
    )(one, two, rest)


def solution(mesh):
    spec = P("prow", "pcol")
    return jax.shard_map(
        on_device,
        mesh=mesh,
        in_specs=(spec,) * 6 + (P(), P()),
        out_specs=(spec,) * 5,
        check_vma=False,
    )
```

```python
import functools

import jax
import jax.numpy as jnp
from jax import lax
from jax.experimental import pallas as pl
from jax.experimental.pallas import tpu as pltpu
from jax.sharding import PartitionSpec as P

MESH = pl.DeviceIdType.MESH
EXACT = lax.Precision.HIGHEST
F32 = jnp.float32
DIMS = (4, 4, 4, 2, 2)


def mm(a, b):
    return jnp.dot(a, b, precision=EXACT, preferred_element_type=F32)


def mm_t(a, b):
    return lax.dot_general(
        a, b, (((0,), (0,)), ((), ())), precision=EXACT, preferred_element_type=F32
    )


def kernel(
    cfg,
    sets_one, sets_two, top, panel_one, panel_two, parent, pivot_one, pivot_two,
    out1_in, out2_in, fin_in,
    arows, zs, packed, landed, grid, bundle, lg, l1, l2, pf,
    acc1, acc2, low1, low2, dir2, upper, b2s, part, sibpart, comb, sums, fin,
    swap_sem, a_send, a_recv, b_send, b_recv, c_send, c_recv,
    ring_send, ring_recv, sib_send, sib_recv, own_sem,
    x_send, x_recv, s_send, s_recv, o1_send, o1_recv, o2_send, o2_recv, back_sem,
):
    B, S1, S2 = cfg
    nx, ny, nzh, nzl, nk = DIMS
    nz = nzh * nzl
    nr = nz * nk
    nc = nx * ny
    sub = B // nr
    H = max(B // 128, 1)
    LN = B // H
    npc = S1 * S1 * H
    share1 = S1 * sub
    share2 = S2 * sub
    gathered = share1 + 2 * share2 + 2 * sub
    half = gathered // 2
    nbr, nbc = top.shape[0], top.shape[3]
    prow = lax.axis_index("prow")
    pcol = lax.axis_index("pcol")
    div, rem = lax.div, lax.rem
    zh, y = div(prow, ny), rem(prow, ny)
    zl, x, core = div(pcol, nx * nk), rem(div(pcol, nk), nx), rem(pcol, nk)
    z = zh * nzl + zl
    line = x * ny + y
    spot = z * nk + core
    y_hi, y_lo = div(y, nk), rem(y, nk)
    turn = y_lo if nzl == 2 else y_lo * 0

    def flip(a, b):
        return a + b - 2 * a * b

    def virtual(zz):
        return zz + turn * (1 - 2 * rem(zz, 2)) if nzl == 2 else zz

    zeta = virtual(z)
    me = zeta * nk + core

    def device(x, y, z, core):
        return (div(z, nzl) * ny + y, rem(z, nzl) * (nx * nk) + x * nk + core)

    def to_member(m):
        return device(x, y, virtual(div(m, nk)), rem(m, nk))

    def to_spot(m):
        return device(x, y, div(m, nk), rem(m, nk))

    def share_of(zz, k):
        return virtual(zz) * nk + k

    def node_of(dx, dy):
        return div(dy, nk) * (nx * nk) + dx * nk + rem(dy, nk)

    taker = device(x, zl * nk + core, zh * nzl + (flip(y_hi, core) if nzl == 2 else y_hi), y_lo)
    holder = device(x, (flip(zl, y_lo) if nzl == 2 else zl) * nk + core, zh * nzl + y_hi, y_lo)
    home = zl * nk + core
    abroad = lax.min(lax.abs(y - home), 1)
    apart = lax.min(abroad + (core if nzl == 2 else core * 0), 1)
    away = apart == 1
    sibling = device(x, y, z, 1 - core)

    if nx == 4 and ny == 4:
        near = [(1, 0), (3, 0), (0, 1), (0, 3), (1, 1), (3, 3), (1, 3), (3, 1),
                (2, 0), (0, 2), (2, 1), (2, 3), (1, 2), (3, 2), (2, 2)]
    else:
        near = [(i, j) for i in range(nx) for j in range(ny) if i + j > 0]

    def shift(k):
        dx = near[k][0] + core * (near[nc - 2 - k][0] - near[k][0])
        dy = near[k][1] + core * (near[nc - 2 - k][1] - near[k][1])
        return rem(x + dx, nx), rem(y + dy, ny), dx * ny + dy

    def each(n, f):
        def body(k, _):
            f(k)
            return 0
        lax.fori_loop(0, n, body, 0)

    def rcopy(src, dst, ss, rs, dev):
        return pltpu.make_async_remote_copy(
            src_ref=src, dst_ref=dst, send_sem=ss, recv_sem=rs, device_id=dev, device_id_type=MESH
        )

    barrier = pltpu.get_barrier_semaphore()

    def greet(dev):
        pl.semaphore_signal(barrier, inc=1, device_id=dev, device_id_type=MESH)

    for dz in range(nz):
        for dk in range(nk):
            if dz + dk > 0:
                greet(device(x, y, rem(z + dz, nz), rem(core + dk, nk)))
    for dx, dy in near:
        greet(device(rem(x + dx, nx), rem(y + dy, ny), z, core))

    for dz in range(nz):
        for dk in range(nk):
            dev = device(x, home, rem(z + dz, nz), rem(core + dk, nk))
            if dz + dk > 0:
                greet(dev)
            else:
                @pl.when(abroad == 1)
                def _():
                    greet(dev)

    @pl.when(away)
    def _():
        greet(holder)

    bundle[0:share1, :] = panel_one[...]
    at = share1
    for ch in range(2):
        bundle[at : at + share2, :] = panel_two[:, ch * B : (ch + 1) * B]
        at += share2
    for ch in range(2):
        bundle[at : at + sub, :] = parent[:, ch * B : (ch + 1) * B]
        at += sub
    bundle[at : at + sub, :] = pivot_one[...]
    at += sub
    for ch in range(2):
        bundle[at : at + sub, :] = pivot_two[:, ch * B : (ch + 1) * B]
        at += sub

    pl.semaphore_wait(barrier, 2 * nr + nc - 3 + abroad + apart)

    def swap_copy(piece):
        rows = pl.ds(0, half) if piece == 0 else pl.ds(half, gathered + 3 * sub - half)
        return rcopy(bundle.at[rows], lg.at[prow, rows], swap_sem.at[0, piece], swap_sem.at[1, piece], taker)

    @pl.when(away)
    def _():
        for piece in range(2):
            swap_copy(piece).start()

    def a_copy(k):
        d = rem(spot + k + 1, nr)
        return rcopy(top.at[:, d], arows.at[pl.ds(spot * nbr, nbr)], a_send.at[k], a_recv.at[k], to_spot(d))

    each(nr - 1, lambda k: a_copy(k).start())
    own_a = pltpu.make_async_copy(top.at[:, spot], arows.at[pl.ds(spot * nbr, nbr)], own_sem.at[0])
    own_a.start()

    steps = nz // 2
    STREAMS = [(1, 0), (-1, 1), (1, 1), (-1, 0)]

    def length(way, piece):
        return steps if (way == 1) == (piece == 0) else steps - 1

    def ring_copy(way, piece, s):
        to = rem(z + way + nz, nz)
        owner = share_of(rem(z - way * s + nz, nz), core)
        ref = lg.at[owner, pl.ds(piece * half, half)]
        w = 0 if way == 1 else 1
        return rcopy(ref, ref, ring_send.at[w, piece, s], ring_recv.at[w, piece, s], device(x, y, to, core))

    def sib_copy(way, piece, s):
        owner = share_of(rem(z - way * s + nz, nz), core)
        ref = lg.at[owner, pl.ds(piece * half, half)]
        w = 0 if way == 1 else 1
        return rcopy(ref, ref, sib_send.at[w, piece, s], sib_recv.at[w, piece, s], sibling)

    def pass_on(s):
        for way, piece in STREAMS:
            n = length(way, piece)
            if s <= n:
                ring_copy(way, piece, s - 1).wait_recv()
                if s < n:
                    ring_copy(way, piece, s).start()
                sib_copy(way, piece, s).start()

    own_a.wait()
    each(nr - 1, lambda k: a_copy(k).wait_recv())

    nb = nr * nbr

    def b_copy(k):
        dx, dy, n = shift(k)
        return rcopy(
            arows.at[:, dx * ny + dy], zs.at[pl.ds(line * nb, nb)], b_send.at[n], b_recv.at[n], device(dx, dy, z, core)
        )

    for k in range(nc - 1):
        b_copy(k).start()
    own_b = pltpu.make_async_copy(arows.at[:, line], zs.at[pl.ds(line * nb, nb)], own_sem.at[1])
    own_b.start()

    @pl.when(jnp.logical_not(away))
    def _():
        lg[prow] = bundle[...]

    for piece in range(2):
        @pl.when(away)
        def _():
            swap_copy(piece).wait_recv()

        for way, part_of in STREAMS:
            if part_of == piece and length(way, piece) > 0:
                ring_copy(way, piece, 0).start()
        sib_copy(1, piece, 0).start()

    pass_on(1)

    own_b.wait()
    for k in range(nc - 1):
        b_copy(k).wait_recv()

    def pack(dx, dy):
        d = dx * ny + dy
        j = node_of(dx, dy)
        cols = []
        for s in range(S1):
            q = sets_one[j, s]
            c = div(q, nbc)
            cc = div(c, nk)
            cols.append((rem(cc, nx) * (ny * nb) + div(cc, nx) * (nk * nbr) + rem(c, nk) * nbr, rem(q, nbc)))

        def row(a):
            p = sets_one[j, a]
            r = div(p, nbr)
            at = rem(r, ny) * nb + div(r, ny) * (nzl * nk * nbr) + rem(p, nbr)
            for b in range(S1):
                packed[d, pl.ds((a * S1 + b) * H, H), :] = zs[at + cols[b][0], cols[b][1]]

        each(S1, row)

    def c_copy(k):
        dx, dy, n = shift(k)
        return rcopy(
            packed.at[dx * ny + dy], landed.at[pl.ds(line * npc, npc)], c_send.at[n], c_recv.at[n],
            device(dx, dy, z, core),
        )

    for k in range(nc - 1):
        pack(*shift(k)[:2])
        c_copy(k).start()
    pack(x, y)
    own_c = pltpu.make_async_copy(packed.at[line], landed.at[pl.ds(line * npc, npc)], own_sem.at[2])
    own_c.start()

    for s in range(2, steps + 1):
        pass_on(s)

    for piece in range(2):
        sib_copy(1, piece, 0).wait_recv()
    for s in range(1, steps + 1):
        for way, piece in STREAMS:
            if s <= length(way, piece):
                sib_copy(way, piece, s).wait_recv()

    def spread(m):
        l1[pl.ds(m * share1, share1), :] = lg[m, 0:share1, :]
        for ch in range(2):
            o = share1 + ch * share2
            l2[ch, pl.ds(m * share2, share2), :] = lg[m, o : o + share2, :]
            o = share1 + 2 * share2 + ch * sub
            pf[ch, pl.ds(m * sub, sub), :] = lg[m, o : o + sub, :]

    each(nr, spread)

    own_c.wait()
    for k in range(nc - 1):
        c_copy(k).wait_recv()

    def assemble(b):
        for a in range(S1):
            for h in range(H):
                i = (a * S1 + b) * H + h
                grid[b, a * sub : (a + 1) * sub, h * LN : (h + 1) * LN] = landed[pl.ds(i, nc, stride=npc), :]

    each(S1, assemble)

    acc1[...] = jnp.zeros_like(acc1)

    def step_one(b):
        acc1[...] -= mm(grid[b], l1[pl.ds(pl.multiple_of(b * B, B), B), :]).reshape(acc1.shape)

    each(S1, step_one)

    def holder_of(m):
        return device(x, rem(m, ny), div(m, ny) * nzl + y_hi, y_lo)

    def o1_copy(a):
        g = a * nr + spot
        return div(g, S1), rcopy(
            acc1.at[a], out1_in.at[pl.ds(rem(g, S1) * sub, sub)],
            o1_send.at[a], o1_recv.at[rem(g, S1)], holder_of(div(g, S1)),
        )

    def o2_copy(t):
        g = t * nr + spot
        return div(g, S2), rcopy(
            b2s.at[t], out2_in.at[pl.ds(rem(g, S2) * sub, sub)],
            o2_send.at[t], o2_recv.at[rem(g, S2)], holder_of(div(g, S2)),
        )

    def stays(d):
        return lax.min(lax.abs(d - prow) + abroad, 1) == 0

    def send_out(n, copy, src, dst):
        def go(a):
            d, cp = copy(a)

            @pl.when(jnp.logical_not(stays(d)))
            def _():
                cp.start()

            @pl.when(stays(d))
            def _():
                at = rem(a * nr + spot, n) * sub
                dst[pl.ds(pl.multiple_of(at, sub), sub), :] = src[a]

        each(n, go)

    def take_out(n, src, dst, send, recv):
        def go(a):
            m = rem(prow * n + a, nr)

            @pl.when(lax.min(lax.abs(m - spot) + abroad, 1) == 1)
            def _():
                rcopy(
                    src.at[0], dst.at[pl.ds(a * sub, sub)], send.at[a], recv.at[a],
                    device(x, home, div(m, nk), rem(m, nk)),
                ).wait_recv()

        each(n, go)

    def done_out(n, copy):
        def go(a):
            d, cp = copy(a)

            @pl.when(jnp.logical_not(stays(d)))
            def _():
                cp.wait_send()

        each(n, go)

    send_out(S1, o1_copy, acc1, out1_in)

    def x_copy(g, cs):
        return rcopy(part.at[:, 1 - core, :, cs], sibpart.at[:, :, cs], x_send.at[g], x_recv.at[g], sibling)

    def s_copy(g, cs, k):
        d = rem(zeta + k + 1, nz)
        return rcopy(
            comb.at[d, :, cs], sums.at[zeta, :, cs], s_send.at[g, k], s_recv.at[g, k], device(x, y, virtual(d), core)
        )

    spans = [pl.ds(0, B), pl.ds(B, 2 * B), pl.ds(3 * B, 2 * B)]

    def combine(g):
        cs = spans[g]
        x_copy(g, cs).wait_recv()
        comb[:, :, cs] = part[:, core, :, cs] + sibpart[:, :, cs]
        for k in range(nz - 1):
            s_copy(g, cs, k).start()

    node = node_of(x, y)
    for a in range(S1):
        low1[a * sub : (a + 1) * sub, :] = l1[pl.ds(pl.multiple_of(a * B + spot * sub, sub), sub), :]
    square = mm_t(low1[...], acc1[...].reshape(S1 * sub, B))
    part[:, :, :, 0:B] = square.reshape(nz, nk, sub, B)
    x_copy(0, spans[0]).start()
    pivot1 = lg[me, gathered : gathered + sub, :]

    for ch in range(2):
        for t in range(S2):
            low2[t * sub : (t + 1) * sub, :] = l2[ch, pl.ds(pl.multiple_of(t * B + spot * sub, sub), sub), :]
        pos = []
        for t in range(S2):
            want = sets_two[2 * node + ch, t]
            at = 0
            for s in range(S1):
                at = at + s * (1 - lax.min(lax.abs(sets_one[node, s] - want), 1))
            pos.append(lax.min(at, S1 - 1))
        acc2[...] = jnp.zeros_like(acc2)
        for t in range(S2):
            acc2[...] += mm(grid[pos[t]], l2[ch, t * B : (t + 1) * B, :]).reshape(acc2.shape)
        for t in range(S2):
            dir2[t * sub : (t + 1) * sub, :] = acc2[pos[t]]
            upper[t * sub : (t + 1) * sub, :] = acc1[pos[t]]
        pc = pf[ch]
        u = upper[...]
        l2c = low2[...]
        b2 = -(dir2[...] + mm(u, pc))
        b2s[:, :, ch * B : (ch + 1) * B] = b2.reshape(S2, sub, B)
        cross = mm_t(u, l2c)
        inner = cross - mm(part[:, :, :, 0:B].reshape(B, B), pc)
        mine = pf[ch, pl.ds(pl.multiple_of(me * sub, sub), sub), :]
        last = mm_t(pc, inner) - mm_t(l2c, b2) + mm_t(mine, mm(pivot1, pc))
        o = B + 2 * ch * B
        part[:, :, :, o : o + B] = cross.reshape(nz, nk, sub, B)
        part[:, :, :, o + B : o + 2 * B] = last.reshape(nz, nk, sub, B)
        x_copy(ch + 1, spans[ch + 1]).start()
        combine(ch)

    combine(2)
    send_out(S2, o2_copy, b2s, out2_in)

    for g in range(3):
        for k in range(nz - 1):
            s_copy(g, spans[g], k).wait_recv()

    total = comb[zeta]
    for k in range(1, nz):
        total = total + sums[rem(zeta + k, nz)]
    corner = pivot1 - total[:, 0:B]
    fin[:, 0:B] = corner
    for ch in range(2):
        o = B + 2 * ch * B
        p2 = gathered + sub + ch * sub
        fin[:, (1 + ch) * B : (2 + ch) * B] = -(mm(corner, pf[ch]) + total[:, o : o + B])
        fin[:, (3 + ch) * B : (4 + ch) * B] = lg[me, p2 : p2 + sub, :] + total[:, o + B : o + 2 * B]

    back = rcopy(fin, fin_in, back_sem.at[0], back_sem.at[1], holder)

    @pl.when(away)
    def _():
        back.start()

    take_out(S1, acc1, out1_in, o1_send, o1_recv)
    take_out(S2, b2s, out2_in, o2_send, o2_recv)

    @pl.when(away)
    def _():
        back.wait_recv()

    @pl.when(jnp.logical_not(away))
    def _():
        fin_in[...] = fin[...]

    @pl.when(away)
    def _():
        for piece in range(2):
            swap_copy(piece).wait_send()
        back.wait_send()

    each(nr - 1, lambda k: a_copy(k).wait_send())
    for k in range(nc - 1):
        b_copy(k).wait_send()
        c_copy(k).wait_send()
    for way, piece in STREAMS:
        for s in range(length(way, piece)):
            ring_copy(way, piece, s).wait_send()
            sib_copy(way, piece, s + 1).wait_send()
    for piece in range(2):
        sib_copy(1, piece, 0).wait_send()
    for g in range(3):
        x_copy(g, spans[g]).wait_send()
        for k in range(nz - 1):
            s_copy(g, spans[g], k).wait_send()
    done_out(S1, o1_copy)
    done_out(S2, o2_copy)


def deliver(one, two, rest, below_one, corner_one, below_two, beside, corner_two):
    B = one.shape[1]
    below_one[...] = one[...]
    below_two[...] = two[...]
    corner_one[...] = rest[:, 0:B]
    beside[...] = rest[:, B : 3 * B]
    corner_two[...] = rest[:, 3 * B : 5 * B]


def on_device(top, panel_one, panel_two, parent, pivot_one, pivot_two, sets_one, sets_two):
    nx, ny, nzh, nzl, nk = DIMS
    nz = nzh * nzl
    nr = nz * nk
    nc = nx * ny
    S1 = sets_one.shape[1]
    S2 = sets_two.shape[1]
    B = panel_one.shape[1]
    sub = B // nr
    H = max(B // 128, 1)
    LN = B // H
    nbr, nbc = top.shape[0] // B, top.shape[1] // B
    npc = S1 * S1 * H
    share1, share2 = S1 * sub, S2 * sub
    gathered = share1 + 2 * share2 + 2 * sub
    whole = gathered + 3 * sub
    steps = nz // 2
    cfg = (B, S1, S2)
    top = top.reshape(nbr, nr, sub, nbc, H, LN)
    vmem = pl.BlockSpec(memory_space=pltpu.VMEM)
    smem = pl.BlockSpec(memory_space=pltpu.SMEM)
    V = lambda *s: pltpu.VMEM(s, F32)
    D = lambda *s: pltpu.SemaphoreType.DMA(s)
    out = lambda *s: jax.ShapeDtypeStruct(s, F32)
    one, two, rest = pl.pallas_call(
        functools.partial(kernel, cfg),
        out_shape=(out(share1, B), out(share2, 2 * B), out(sub, 5 * B)),
        in_specs=[smem, smem] + [vmem] * 6,
        out_specs=(vmem,) * 3,
        scratch_shapes=[
            V(nr * nbr, sub, nbc, H, LN),
            V(nc * nr * nbr, nbc, H, LN),
            V(nc, npc, LN),
            V(nc * npc, LN),
            V(S1, share1, B),
            V(whole, B),
            V(nr, whole, B),
            V(S1 * B, B),
            V(2, S2 * B, B),
            V(2, B, B),
            V(S1, sub, B),
            V(S1, sub, B),
            V(share1, B),
            V(share2, B),
            V(share2, B),
            V(share2, B),
            V(S2, sub, 2 * B),
            V(nz, nk, sub, 5 * B),
            V(nz, sub, 5 * B),
            V(nz, sub, 5 * B),
            V(nz, sub, 5 * B),
            V(sub, 5 * B),
            D(2, 2),
            D(nr - 1), D(nr - 1), D(nc), D(nc), D(nc), D(nc),
            D(2, 2, steps), D(2, 2, steps), D(2, 2, steps + 1), D(2, 2, steps + 1), D(3),
            D(3), D(3), D(3, nz - 1), D(3, nz - 1), D(S1), D(S1), D(S2), D(S2), D(2),
        ],
        compiler_params=pltpu.CompilerParams(
            collective_id=0, has_side_effects=True, vmem_limit_bytes=56 * 1024 * 1024
        ),
    )(sets_one, sets_two, top, panel_one, panel_two, parent, pivot_one, pivot_two)
    return pl.pallas_call(
        deliver,
        out_shape=(out(share1, B), out(sub, B), out(share2, 2 * B), out(sub, 2 * B), out(sub, 2 * B)),
        in_specs=[vmem] * 3,
        out_specs=(vmem,) * 5,
    )(one, two, rest)


def solution(mesh):
    spec = P("prow", "pcol")
    return jax.shard_map(
        on_device,
        mesh=mesh,
        in_specs=(spec,) * 6 + (P(), P()),
        out_specs=(spec,) * 5,
        check_vma=False,
    )
```

```python
import functools

import jax
import jax.numpy as jnp
from jax import lax
from jax.experimental import pallas as pl
from jax.experimental.pallas import tpu as pltpu
from jax.sharding import PartitionSpec as P

MESH = pl.DeviceIdType.MESH
EXACT = lax.Precision.HIGHEST
F32 = jnp.float32
DIMS = (4, 4, 4, 2, 2)


def mm(a, b):
    return jnp.dot(a, b, precision=EXACT, preferred_element_type=F32)


def mm_t(a, b):
    return lax.dot_general(
        a, b, (((0,), (0,)), ((), ())), precision=EXACT, preferred_element_type=F32
    )


def kernel(
    cfg,
    sets_one, sets_two, top, panel_one, panel_two, parent, pivot_one, pivot_two,
    out1_in, out2_in, fin_in,
    arows, zs, packed, landed, grid, bundle, lg, l1, l2, pf,
    acc1, acc2, low1, low2, dir2, upper, b2s, part, sibpart, comb, sums, fin,
    swap_sem, a_send, a_recv, b_send, b_recv, c_send, c_recv,
    ring_send, ring_recv, sib_send, sib_recv, own_sem,
    x_send, x_recv, s_send, s_recv, o1_send, o1_recv, o2_send, o2_recv, back_sem,
):
    B, S1, S2 = cfg
    nx, ny, nzh, nzl, nk = DIMS
    nz = nzh * nzl
    nr = nz * nk
    nc = nx * ny
    sub = B // nr
    H = max(B // 128, 1)
    LN = B // H
    npc = S1 * S1 * H
    share1 = S1 * sub
    share2 = S2 * sub
    gathered = share1 + 2 * share2 + 2 * sub
    half = gathered // 2
    nbr, nbc = top.shape[0], top.shape[3]
    prow = lax.axis_index("prow")
    pcol = lax.axis_index("pcol")
    div, rem = lax.div, lax.rem
    zh, y = div(prow, ny), rem(prow, ny)
    zl, x, core = div(pcol, nx * nk), rem(div(pcol, nk), nx), rem(pcol, nk)
    z = zh * nzl + zl
    line = x * ny + y
    spot = z * nk + core
    y_hi, y_lo = div(y, nk), rem(y, nk)
    turn = y_lo if nzl == 2 else y_lo * 0

    def flip(a, b):
        return a + b - 2 * a * b

    def virtual(zz):
        return zz + turn * (1 - 2 * rem(zz, 2)) if nzl == 2 else zz

    zeta = virtual(z)
    me = zeta * nk + core

    def device(x, y, z, core):
        return (div(z, nzl) * ny + y, rem(z, nzl) * (nx * nk) + x * nk + core)

    def to_member(m):
        return device(x, y, virtual(div(m, nk)), rem(m, nk))

    def to_spot(m):
        return device(x, y, div(m, nk), rem(m, nk))

    def share_of(zz, k):
        return virtual(zz) * nk + k

    def node_of(dx, dy):
        return div(dy, nk) * (nx * nk) + dx * nk + rem(dy, nk)

    taker = device(x, zl * nk + core, zh * nzl + (flip(y_hi, core) if nzl == 2 else y_hi), y_lo)
    holder = device(x, (flip(zl, y_lo) if nzl == 2 else zl) * nk + core, zh * nzl + y_hi, y_lo)
    home = zl * nk + core
    abroad = lax.min(lax.abs(y - home), 1)
    apart = lax.min(abroad + (core if nzl == 2 else core * 0), 1)
    away = apart == 1
    sibling = device(x, y, z, 1 - core)

    if nx == 4 and ny == 4:
        near = [(1, 0), (3, 0), (0, 1), (0, 3), (1, 1), (3, 3), (1, 3), (3, 1),
                (2, 0), (0, 2), (2, 1), (2, 3), (1, 2), (3, 2), (2, 2)]
    else:
        near = [(i, j) for i in range(nx) for j in range(ny) if i + j > 0]

    def shift(k):
        dx = near[k][0] + core * (near[nc - 2 - k][0] - near[k][0])
        dy = near[k][1] + core * (near[nc - 2 - k][1] - near[k][1])
        return rem(x + dx, nx), rem(y + dy, ny), dx * ny + dy

    def each(n, f):
        def body(k, _):
            f(k)
            return 0
        lax.fori_loop(0, n, body, 0)

    def rcopy(src, dst, ss, rs, dev):
        return pltpu.make_async_remote_copy(
            src_ref=src, dst_ref=dst, send_sem=ss, recv_sem=rs, device_id=dev, device_id_type=MESH
        )

    barrier = pltpu.get_barrier_semaphore()

    def greet(dev):
        pl.semaphore_signal(barrier, inc=1, device_id=dev, device_id_type=MESH)

    for dz in range(nz):
        for dk in range(nk):
            if dz + dk > 0:
                greet(device(x, y, rem(z + dz, nz), rem(core + dk, nk)))
    for dx, dy in near:
        greet(device(rem(x + dx, nx), rem(y + dy, ny), z, core))

    for dz in range(nz):
        for dk in range(nk):
            dev = device(x, home, rem(z + dz, nz), rem(core + dk, nk))
            if dz + dk > 0:
                greet(dev)
            else:
                @pl.when(abroad == 1)
                def _():
                    greet(dev)

    @pl.when(away)
    def _():
        greet(holder)

    bundle[0:share1, :] = panel_one[...]
    at = share1
    for ch in range(2):
        bundle[at : at + share2, :] = panel_two[:, ch * B : (ch + 1) * B]
        at += share2
    for ch in range(2):
        bundle[at : at + sub, :] = parent[:, ch * B : (ch + 1) * B]
        at += sub
    bundle[at : at + sub, :] = pivot_one[...]
    at += sub
    for ch in range(2):
        bundle[at : at + sub, :] = pivot_two[:, ch * B : (ch + 1) * B]
        at += sub

    pl.semaphore_wait(barrier, 2 * nr + nc - 3 + abroad + apart)

    def swap_copy(piece):
        rows = pl.ds(0, half) if piece == 0 else pl.ds(half, gathered + 3 * sub - half)
        return rcopy(bundle.at[rows], lg.at[prow, rows], swap_sem.at[0, piece], swap_sem.at[1, piece], taker)

    @pl.when(away)
    def _():
        for piece in range(2):
            swap_copy(piece).start()

    def a_copy(k, part_of):
        d = rem(spot + k + 1, nr)
        return rcopy(
            top.at[part_of, d], arows.at[part_of, spot], a_send.at[part_of, k], a_recv.at[part_of, k], to_spot(d)
        )

    for i in range(nbr):
        each(nr - 1, lambda k: a_copy(k, i).start())
    own_a = pltpu.make_async_copy(top.at[:, spot], arows.at[:, spot], own_sem.at[0])
    own_a.start()

    steps = nz // 2
    STREAMS = [(1, 0), (-1, 1), (1, 1), (-1, 0)]

    def length(way, piece):
        return steps if (way == 1) == (piece == 0) else steps - 1

    def ring_copy(way, piece, s):
        to = rem(z + way + nz, nz)
        owner = share_of(rem(z - way * s + nz, nz), core)
        ref = lg.at[owner, pl.ds(piece * half, half)]
        w = 0 if way == 1 else 1
        return rcopy(ref, ref, ring_send.at[w, piece, s], ring_recv.at[w, piece, s], device(x, y, to, core))

    def sib_copy(way, piece, s):
        owner = share_of(rem(z - way * s + nz, nz), core)
        ref = lg.at[owner, pl.ds(piece * half, half)]
        w = 0 if way == 1 else 1
        return rcopy(ref, ref, sib_send.at[w, piece, s], sib_recv.at[w, piece, s], sibling)

    def pass_on(s):
        for way, piece in STREAMS:
            n = length(way, piece)
            if s <= n:
                ring_copy(way, piece, s - 1).wait_recv()
                if s < n:
                    ring_copy(way, piece, s).start()
                sib_copy(way, piece, s).start()

    own_a.wait()

    nb = nr * nbr

    def b_copy(k, part_of):
        dx, dy, n = shift(k)
        return rcopy(
            arows.at[part_of, :, dx * ny + dy], zs.at[pl.ds((line * nbr + part_of) * nr, nr)],
            b_send.at[part_of, n], b_recv.at[part_of, n], device(dx, dy, z, core),
        )

    own_b = [
        pltpu.make_async_copy(
            arows.at[i, :, line], zs.at[pl.ds((line * nbr + i) * nr, nr)], own_sem.at[1 + i]
        )
        for i in range(nbr)
    ]
    for i in range(nbr):
        each(nr - 1, lambda k: a_copy(k, i).wait_recv())
        for k in range(nc - 1):
            b_copy(k, i).start()
        own_b[i].start()

    @pl.when(jnp.logical_not(away))
    def _():
        lg[prow] = bundle[...]

    for piece in range(2):
        @pl.when(away)
        def _():
            swap_copy(piece).wait_recv()

        for way, part_of in STREAMS:
            if part_of == piece and length(way, piece) > 0:
                ring_copy(way, piece, 0).start()
        sib_copy(1, piece, 0).start()

    pass_on(1)

    for i in range(nbr):
        own_b[i].wait()
        for k in range(nc - 1):
            b_copy(k, i).wait_recv()

    def pack(dx, dy):
        d = dx * ny + dy
        j = node_of(dx, dy)
        cols = []
        for s in range(S1):
            q = sets_one[j, s]
            c = div(q, nbc)
            cc = div(c, nk)
            cols.append((rem(cc, nx) * (ny * nb) + div(cc, nx) * nk + rem(c, nk), rem(q, nbc)))

        def row(a):
            p = sets_one[j, a]
            r = div(p, nbr)
            at = rem(r, ny) * nb + rem(p, nbr) * nr + div(r, ny) * (nzl * nk)
            for b in range(S1):
                packed[d, pl.ds((a * S1 + b) * H, H), :] = zs[at + cols[b][0], cols[b][1]]

        each(S1, row)

    def c_copy(k):
        dx, dy, n = shift(k)
        return rcopy(
            packed.at[dx * ny + dy], landed.at[pl.ds(line * npc, npc)], c_send.at[n], c_recv.at[n],
            device(dx, dy, z, core),
        )

    for k in range(nc - 1):
        pack(*shift(k)[:2])
        c_copy(k).start()
    pack(x, y)
    own_c = pltpu.make_async_copy(packed.at[line], landed.at[pl.ds(line * npc, npc)], own_sem.at[1 + nbr])
    own_c.start()

    for s in range(2, steps + 1):
        pass_on(s)

    for piece in range(2):
        sib_copy(1, piece, 0).wait_recv()
    for s in range(1, steps + 1):
        for way, piece in STREAMS:
            if s <= length(way, piece):
                sib_copy(way, piece, s).wait_recv()

    def spread(m):
        l1[pl.ds(m * share1, share1), :] = lg[m, 0:share1, :]
        for ch in range(2):
            o = share1 + ch * share2
            l2[ch, pl.ds(m * share2, share2), :] = lg[m, o : o + share2, :]
            o = share1 + 2 * share2 + ch * sub
            pf[ch, pl.ds(m * sub, sub), :] = lg[m, o : o + sub, :]

    each(nr, spread)

    own_c.wait()
    for k in range(nc - 1):
        c_copy(k).wait_recv()

    def assemble(b):
        for a in range(S1):
            for h in range(H):
                i = (a * S1 + b) * H + h
                grid[b, a * sub : (a + 1) * sub, h * LN : (h + 1) * LN] = landed[pl.ds(i, nc, stride=npc), :]

    each(S1, assemble)

    acc1[...] = jnp.zeros_like(acc1)

    def step_one(b):
        acc1[...] -= mm(grid[b], l1[pl.ds(pl.multiple_of(b * B, B), B), :]).reshape(acc1.shape)

    each(S1, step_one)

    def holder_of(m):
        return device(x, rem(m, ny), div(m, ny) * nzl + y_hi, y_lo)

    def o1_copy(a):
        g = a * nr + spot
        return div(g, S1), rcopy(
            acc1.at[a], out1_in.at[pl.ds(rem(g, S1) * sub, sub)],
            o1_send.at[a], o1_recv.at[rem(g, S1)], holder_of(div(g, S1)),
        )

    def o2_copy(t):
        g = t * nr + spot
        return div(g, S2), rcopy(
            b2s.at[t], out2_in.at[pl.ds(rem(g, S2) * sub, sub)],
            o2_send.at[t], o2_recv.at[rem(g, S2)], holder_of(div(g, S2)),
        )

    def stays(d):
        return lax.min(lax.abs(d - prow) + abroad, 1) == 0

    def send_out(n, copy, src, dst):
        def go(a):
            d, cp = copy(a)

            @pl.when(jnp.logical_not(stays(d)))
            def _():
                cp.start()

            @pl.when(stays(d))
            def _():
                at = rem(a * nr + spot, n) * sub
                dst[pl.ds(pl.multiple_of(at, sub), sub), :] = src[a]

        each(n, go)

    def take_out(n, src, dst, send, recv):
        def go(a):
            m = rem(prow * n + a, nr)

            @pl.when(lax.min(lax.abs(m - spot) + abroad, 1) == 1)
            def _():
                rcopy(
                    src.at[0], dst.at[pl.ds(a * sub, sub)], send.at[a], recv.at[a],
                    device(x, home, div(m, nk), rem(m, nk)),
                ).wait_recv()

        each(n, go)

    def done_out(n, copy):
        def go(a):
            d, cp = copy(a)

            @pl.when(jnp.logical_not(stays(d)))
            def _():
                cp.wait_send()

        each(n, go)

    send_out(S1, o1_copy, acc1, out1_in)

    def x_copy(g, cs):
        return rcopy(part.at[:, 1 - core, :, cs], sibpart.at[:, :, cs], x_send.at[g], x_recv.at[g], sibling)

    def s_copy(g, cs, k):
        d = rem(zeta + k + 1, nz)
        return rcopy(
            comb.at[d, :, cs], sums.at[zeta, :, cs], s_send.at[g, k], s_recv.at[g, k], device(x, y, virtual(d), core)
        )

    spans = [pl.ds(0, B), pl.ds(B, 2 * B), pl.ds(3 * B, 2 * B)]

    def combine(g):
        cs = spans[g]
        x_copy(g, cs).wait_recv()
        comb[:, :, cs] = part[:, core, :, cs] + sibpart[:, :, cs]
        for k in range(nz - 1):
            s_copy(g, cs, k).start()

    node = node_of(x, y)
    for a in range(S1):
        low1[a * sub : (a + 1) * sub, :] = l1[pl.ds(pl.multiple_of(a * B + spot * sub, sub), sub), :]
    square = mm_t(low1[...], acc1[...].reshape(S1 * sub, B))
    part[:, :, :, 0:B] = square.reshape(nz, nk, sub, B)
    x_copy(0, spans[0]).start()
    pivot1 = lg[me, gathered : gathered + sub, :]

    for ch in range(2):
        for t in range(S2):
            low2[t * sub : (t + 1) * sub, :] = l2[ch, pl.ds(pl.multiple_of(t * B + spot * sub, sub), sub), :]
        pos = []
        for t in range(S2):
            want = sets_two[2 * node + ch, t]
            at = 0
            for s in range(S1):
                at = at + s * (1 - lax.min(lax.abs(sets_one[node, s] - want), 1))
            pos.append(lax.min(at, S1 - 1))
        acc2[...] = jnp.zeros_like(acc2)
        for t in range(S2):
            acc2[...] += mm(grid[pos[t]], l2[ch, t * B : (t + 1) * B, :]).reshape(acc2.shape)
        for t in range(S2):
            dir2[t * sub : (t + 1) * sub, :] = acc2[pos[t]]
            upper[t * sub : (t + 1) * sub, :] = acc1[pos[t]]
        pc = pf[ch]
        u = upper[...]
        l2c = low2[...]
        b2 = -(dir2[...] + mm(u, pc))
        b2s[:, :, ch * B : (ch + 1) * B] = b2.reshape(S2, sub, B)
        cross = mm_t(u, l2c)
        inner = cross - mm(part[:, :, :, 0:B].reshape(B, B), pc)
        mine = pf[ch, pl.ds(pl.multiple_of(me * sub, sub), sub), :]
        last = mm_t(pc, inner) - mm_t(l2c, b2) + mm_t(mine, mm(pivot1, pc))
        o = B + 2 * ch * B
        part[:, :, :, o : o + B] = cross.reshape(nz, nk, sub, B)
        part[:, :, :, o + B : o + 2 * B] = last.reshape(nz, nk, sub, B)
        x_copy(ch + 1, spans[ch + 1]).start()
        combine(ch)

    combine(2)
    send_out(S2, o2_copy, b2s, out2_in)

    for g in range(3):
        for k in range(nz - 1):
            s_copy(g, spans[g], k).wait_recv()

    total = comb[zeta]
    for k in range(1, nz):
        total = total + sums[rem(zeta + k, nz)]
    corner = pivot1 - total[:, 0:B]
    fin[:, 0:B] = corner
    for ch in range(2):
        o = B + 2 * ch * B
        p2 = gathered + sub + ch * sub
        fin[:, (1 + ch) * B : (2 + ch) * B] = -(mm(corner, pf[ch]) + total[:, o : o + B])
        fin[:, (3 + ch) * B : (4 + ch) * B] = lg[me, p2 : p2 + sub, :] + total[:, o + B : o + 2 * B]

    back = rcopy(fin, fin_in, back_sem.at[0], back_sem.at[1], holder)

    @pl.when(away)
    def _():
        back.start()

    take_out(S1, acc1, out1_in, o1_send, o1_recv)
    take_out(S2, b2s, out2_in, o2_send, o2_recv)

    @pl.when(away)
    def _():
        back.wait_recv()

    @pl.when(jnp.logical_not(away))
    def _():
        fin_in[...] = fin[...]

    @pl.when(away)
    def _():
        for piece in range(2):
            swap_copy(piece).wait_send()
        back.wait_send()

    for i in range(nbr):
        each(nr - 1, lambda k: a_copy(k, i).wait_send())
        for k in range(nc - 1):
            b_copy(k, i).wait_send()
    for k in range(nc - 1):
        c_copy(k).wait_send()
    for way, piece in STREAMS:
        for s in range(length(way, piece)):
            ring_copy(way, piece, s).wait_send()
            sib_copy(way, piece, s + 1).wait_send()
    for piece in range(2):
        sib_copy(1, piece, 0).wait_send()
    for g in range(3):
        x_copy(g, spans[g]).wait_send()
        for k in range(nz - 1):
            s_copy(g, spans[g], k).wait_send()
    done_out(S1, o1_copy)
    done_out(S2, o2_copy)


def deliver(one, two, rest, below_one, corner_one, below_two, beside, corner_two):
    B = one.shape[1]
    below_one[...] = one[...]
    below_two[...] = two[...]
    corner_one[...] = rest[:, 0:B]
    beside[...] = rest[:, B : 3 * B]
    corner_two[...] = rest[:, 3 * B : 5 * B]


def on_device(top, panel_one, panel_two, parent, pivot_one, pivot_two, sets_one, sets_two):
    nx, ny, nzh, nzl, nk = DIMS
    nz = nzh * nzl
    nr = nz * nk
    nc = nx * ny
    S1 = sets_one.shape[1]
    S2 = sets_two.shape[1]
    B = panel_one.shape[1]
    sub = B // nr
    H = max(B // 128, 1)
    LN = B // H
    nbr, nbc = top.shape[0] // B, top.shape[1] // B
    npc = S1 * S1 * H
    share1, share2 = S1 * sub, S2 * sub
    gathered = share1 + 2 * share2 + 2 * sub
    whole = gathered + 3 * sub
    steps = nz // 2
    cfg = (B, S1, S2)
    top = top.reshape(nbr, nr, sub, nbc, H, LN)
    vmem = pl.BlockSpec(memory_space=pltpu.VMEM)
    smem = pl.BlockSpec(memory_space=pltpu.SMEM)
    V = lambda *s: pltpu.VMEM(s, F32)
    D = lambda *s: pltpu.SemaphoreType.DMA(s)
    out = lambda *s: jax.ShapeDtypeStruct(s, F32)
    one, two, rest = pl.pallas_call(
        functools.partial(kernel, cfg),
        out_shape=(out(share1, B), out(share2, 2 * B), out(sub, 5 * B)),
        in_specs=[smem, smem] + [vmem] * 6,
        out_specs=(vmem,) * 3,
        scratch_shapes=[
            V(nbr, nr, sub, nbc, H, LN),
            V(nc * nr * nbr, nbc, H, LN),
            V(nc, npc, LN),
            V(nc * npc, LN),
            V(S1, share1, B),
            V(whole, B),
            V(nr, whole, B),
            V(S1 * B, B),
            V(2, S2 * B, B),
            V(2, B, B),
            V(S1, sub, B),
            V(S1, sub, B),
            V(share1, B),
            V(share2, B),
            V(share2, B),
            V(share2, B),
            V(S2, sub, 2 * B),
            V(nz, nk, sub, 5 * B),
            V(nz, sub, 5 * B),
            V(nz, sub, 5 * B),
            V(nz, sub, 5 * B),
            V(sub, 5 * B),
            D(2, 2),
            D(nbr, nr - 1), D(nbr, nr - 1), D(nbr, nc), D(nbr, nc), D(nc), D(nc),
            D(2, 2, steps), D(2, 2, steps), D(2, 2, steps + 1), D(2, 2, steps + 1), D(2 + nbr),
            D(3), D(3), D(3, nz - 1), D(3, nz - 1), D(S1), D(S1), D(S2), D(S2), D(2),
        ],
        compiler_params=pltpu.CompilerParams(
            collective_id=0, has_side_effects=True, vmem_limit_bytes=56 * 1024 * 1024
        ),
    )(sets_one, sets_two, top, panel_one, panel_two, parent, pivot_one, pivot_two)
    return pl.pallas_call(
        deliver,
        out_shape=(out(share1, B), out(sub, B), out(share2, 2 * B), out(sub, 2 * B), out(sub, 2 * B)),
        in_specs=[vmem] * 3,
        out_specs=(vmem,) * 5,
    )(one, two, rest)


def solution(mesh):
    spec = P("prow", "pcol")
    return jax.shard_map(
        on_device,
        mesh=mesh,
        in_specs=(spec,) * 6 + (P(), P()),
        out_specs=(spec,) * 5,
        check_vma=False,
    )
```

```python
import functools

import jax
import jax.numpy as jnp
from jax import lax
from jax.experimental import pallas as pl
from jax.experimental.pallas import tpu as pltpu
from jax.sharding import PartitionSpec as P

MESH = pl.DeviceIdType.MESH
EXACT = lax.Precision.HIGHEST
F32 = jnp.float32
DIMS = (4, 4, 4, 2, 2)


def mm(a, b):
    return jnp.dot(a, b, precision=EXACT, preferred_element_type=F32)


def mm_t(a, b):
    return lax.dot_general(
        a, b, (((0,), (0,)), ((), ())), precision=EXACT, preferred_element_type=F32
    )


def kernel(
    cfg,
    sets_one, sets_two, top, panel_one, panel_two, parent, pivot_one, pivot_two,
    out1_in, out2_in, fin_in,
    arows, zs, packed, landed, grid, bundle, lg, l1, l2, pf,
    acc1, acc2, low1, low2, dir2, upper, b2s, part, sibpart, comb, sums, fin,
    swap_sem, a_send, a_recv, b_send, b_recv, c_send, c_recv,
    ring_send, ring_recv, sib_send, sib_recv, own_sem,
    x_send, x_recv, s_send, s_recv, o1_send, o1_recv, o2_send, o2_recv, back_sem,
):
    B, S1, S2 = cfg
    nx, ny, nzh, nzl, nk = DIMS
    nz = nzh * nzl
    nr = nz * nk
    nc = nx * ny
    sub = B // nr
    H = max(B // 128, 1)
    LN = B // H
    npc = S1 * S1 * H
    share1 = S1 * sub
    share2 = S2 * sub
    gathered = share1 + 2 * share2 + 2 * sub
    half = gathered // 2
    nbr, nbc = top.shape[0], top.shape[3]
    prow = lax.axis_index("prow")
    pcol = lax.axis_index("pcol")
    div, rem = lax.div, lax.rem
    zh, y = div(prow, ny), rem(prow, ny)
    zl, x, core = div(pcol, nx * nk), rem(div(pcol, nk), nx), rem(pcol, nk)
    z = zh * nzl + zl
    line = x * ny + y
    spot = z * nk + core
    y_hi, y_lo = div(y, nk), rem(y, nk)
    turn = y_lo if nzl == 2 else y_lo * 0

    def flip(a, b):
        return a + b - 2 * a * b

    def virtual(zz):
        return zz + turn * (1 - 2 * rem(zz, 2)) if nzl == 2 else zz

    zeta = virtual(z)
    me = zeta * nk + core

    def device(x, y, z, core):
        return (div(z, nzl) * ny + y, rem(z, nzl) * (nx * nk) + x * nk + core)

    def to_member(m):
        return device(x, y, virtual(div(m, nk)), rem(m, nk))

    def to_spot(m):
        return device(x, y, div(m, nk), rem(m, nk))

    def share_of(zz, k):
        return virtual(zz) * nk + k

    def node_of(dx, dy):
        return div(dy, nk) * (nx * nk) + dx * nk + rem(dy, nk)

    taker = device(x, zl * nk + core, zh * nzl + (flip(y_hi, core) if nzl == 2 else y_hi), y_lo)
    holder = device(x, (flip(zl, y_lo) if nzl == 2 else zl) * nk + core, zh * nzl + y_hi, y_lo)
    home = zl * nk + core
    abroad = lax.min(lax.abs(y - home), 1)
    apart = lax.min(abroad + (core if nzl == 2 else core * 0), 1)
    away = apart == 1
    sibling = device(x, y, z, 1 - core)

    if nx == 4 and ny == 4:
        near = [(1, 0), (3, 0), (0, 1), (0, 3), (1, 1), (3, 3), (1, 3), (3, 1),
                (2, 0), (0, 2), (2, 1), (2, 3), (1, 2), (3, 2), (2, 2)]
    else:
        near = [(i, j) for i in range(nx) for j in range(ny) if i + j > 0]

    def shift(k):
        dx = near[k][0] + core * (near[nc - 2 - k][0] - near[k][0])
        dy = near[k][1] + core * (near[nc - 2 - k][1] - near[k][1])
        return rem(x + dx, nx), rem(y + dy, ny), dx * ny + dy

    def each(n, f):
        def body(k, _):
            f(k)
            return 0
        lax.fori_loop(0, n, body, 0)

    def rcopy(src, dst, ss, rs, dev):
        return pltpu.make_async_remote_copy(
            src_ref=src, dst_ref=dst, send_sem=ss, recv_sem=rs, device_id=dev, device_id_type=MESH
        )

    barrier = pltpu.get_barrier_semaphore()

    def greet(dev):
        pl.semaphore_signal(barrier, inc=1, device_id=dev, device_id_type=MESH)

    for dz in range(nz):
        for dk in range(nk):
            if dz + dk > 0:
                greet(device(x, y, rem(z + dz, nz), rem(core + dk, nk)))
    for dx, dy in near:
        greet(device(rem(x + dx, nx), rem(y + dy, ny), z, core))

    for dz in range(nz):
        for dk in range(nk):
            dev = device(x, home, rem(z + dz, nz), rem(core + dk, nk))
            if dz + dk > 0:
                greet(dev)
            else:
                @pl.when(abroad == 1)
                def _():
                    greet(dev)

    @pl.when(away)
    def _():
        greet(holder)

    bundle[0:share1, :] = panel_one[...]
    at = share1
    for ch in range(2):
        bundle[at : at + share2, :] = panel_two[:, ch * B : (ch + 1) * B]
        at += share2
    for ch in range(2):
        bundle[at : at + sub, :] = parent[:, ch * B : (ch + 1) * B]
        at += sub
    bundle[at : at + sub, :] = pivot_one[...]
    at += sub
    for ch in range(2):
        bundle[at : at + sub, :] = pivot_two[:, ch * B : (ch + 1) * B]
        at += sub

    pl.semaphore_wait(barrier, 2 * nr + nc - 3 + abroad + apart)

    def swap_copy(piece):
        rows = pl.ds(0, half) if piece == 0 else pl.ds(half, gathered + 3 * sub - half)
        return rcopy(bundle.at[rows], lg.at[prow, rows], swap_sem.at[0, piece], swap_sem.at[1, piece], taker)

    @pl.when(away)
    def _():
        for piece in range(2):
            swap_copy(piece).start()

    def a_copy(k, part_of):
        d = rem(spot + k + 1, nr)
        return rcopy(
            top.at[part_of, d], arows.at[part_of, spot], a_send.at[part_of, k], a_recv.at[part_of, k], to_spot(d)
        )

    for i in range(nbr):
        each(nr - 1, lambda k: a_copy(k, i).start())
    own_a = pltpu.make_async_copy(top.at[:, spot], arows.at[:, spot], own_sem.at[0])
    own_a.start()

    steps = nz // 2
    STREAMS = [(1, 0), (-1, 1), (1, 1), (-1, 0)]

    def length(way, piece):
        return steps if (way == 1) == (piece == 0) else steps - 1

    def ring_copy(way, piece, s):
        to = rem(z + way + nz, nz)
        owner = share_of(rem(z - way * s + nz, nz), core)
        ref = lg.at[owner, pl.ds(piece * half, half)]
        w = 0 if way == 1 else 1
        return rcopy(ref, ref, ring_send.at[w, piece, s], ring_recv.at[w, piece, s], device(x, y, to, core))

    def sib_copy(way, piece, s):
        owner = share_of(rem(z - way * s + nz, nz), core)
        ref = lg.at[owner, pl.ds(piece * half, half)]
        w = 0 if way == 1 else 1
        return rcopy(ref, ref, sib_send.at[w, piece, s], sib_recv.at[w, piece, s], sibling)

    def pass_on(s):
        for way, piece in STREAMS:
            n = length(way, piece)
            if s <= n:
                ring_copy(way, piece, s - 1).wait_recv()
                if s < n:
                    ring_copy(way, piece, s).start()
                sib_copy(way, piece, s).start()

    own_a.wait()

    nb = nr * nbr

    def b_copy(k, part_of):
        dx, dy, n = shift(k)
        return rcopy(
            arows.at[part_of, :, dx * ny + dy], zs.at[pl.ds((line * nbr + part_of) * nr, nr)],
            b_send.at[part_of, n], b_recv.at[part_of, n], device(dx, dy, z, core),
        )

    own_b = [
        pltpu.make_async_copy(
            arows.at[i, :, line], zs.at[pl.ds((line * nbr + i) * nr, nr)], own_sem.at[1 + i]
        )
        for i in range(nbr)
    ]
    for i in range(nbr):
        each(nr - 1, lambda k: a_copy(k, i).wait_recv())
        for k in range(nc - 1):
            b_copy(k, i).start()
        own_b[i].start()

    @pl.when(jnp.logical_not(away))
    def _():
        lg[prow] = bundle[...]

    for piece in range(2):
        @pl.when(away)
        def _():
            swap_copy(piece).wait_recv()

        for way, part_of in STREAMS:
            if part_of == piece and length(way, piece) > 0:
                ring_copy(way, piece, 0).start()
        sib_copy(1, piece, 0).start()

    pass_on(1)

    for i in range(nbr):
        own_b[i].wait()
        for k in range(nc - 1):
            b_copy(k, i).wait_recv()

    def pack(dx, dy):
        d = dx * ny + dy
        j = node_of(dx, dy)
        cols = []
        for s in range(S1):
            q = sets_one[j, s]
            c = div(q, nbc)
            cc = div(c, nk)
            cols.append((rem(cc, nx) * (ny * nb) + div(cc, nx) * nk + rem(c, nk), rem(q, nbc)))

        def row(a):
            p = sets_one[j, a]
            r = div(p, nbr)
            at = rem(r, ny) * nb + rem(p, nbr) * nr + div(r, ny) * (nzl * nk)
            for b in range(S1):
                packed[d, pl.ds((a * S1 + b) * H, H), :] = zs[at + cols[b][0], cols[b][1]]

        each(S1, row)

    def c_copy(k):
        dx, dy, n = shift(k)
        return rcopy(
            packed.at[dx * ny + dy], landed.at[pl.ds(line * npc, npc)], c_send.at[n], c_recv.at[n],
            device(dx, dy, z, core),
        )

    for k in range(nc - 1):
        pack(*shift(k)[:2])
        c_copy(k).start()
    pack(x, y)
    own_c = pltpu.make_async_copy(packed.at[line], landed.at[pl.ds(line * npc, npc)], own_sem.at[1 + nbr])
    own_c.start()

    for s in range(2, steps + 1):
        pass_on(s)

    for piece in range(2):
        sib_copy(1, piece, 0).wait_recv()
    for s in range(1, steps + 1):
        for way, piece in STREAMS:
            if s <= length(way, piece):
                sib_copy(way, piece, s).wait_recv()

    def spread(m):
        l1[pl.ds(m * share1, share1), :] = lg[m, 0:share1, :]
        for ch in range(2):
            o = share1 + ch * share2
            l2[ch, pl.ds(m * share2, share2), :] = lg[m, o : o + share2, :]
            o = share1 + 2 * share2 + ch * sub
            pf[ch, pl.ds(m * sub, sub), :] = lg[m, o : o + sub, :]

    each(nr, spread)

    own_c.wait()
    for k in range(nc - 1):
        c_copy(k).wait_recv()

    def assemble(b):
        for a in range(S1):
            for h in range(H):
                i = (a * S1 + b) * H + h
                grid[b, a * sub : (a + 1) * sub, h * LN : (h + 1) * LN] = landed[pl.ds(i, nc, stride=npc), :]

    each(S1, assemble)

    total = mm(grid[0], l1[0:B, :])
    for b in range(1, S1):
        total = total + mm(grid[b], l1[b * B : (b + 1) * B, :])
    acc1[...] = -total.reshape(acc1.shape)

    def holder_of(m):
        return device(x, rem(m, ny), div(m, ny) * nzl + y_hi, y_lo)

    def o1_copy(a):
        g = a * nr + spot
        return div(g, S1), rcopy(
            acc1.at[a], out1_in.at[pl.ds(rem(g, S1) * sub, sub)],
            o1_send.at[a], o1_recv.at[rem(g, S1)], holder_of(div(g, S1)),
        )

    def o2_copy(t):
        g = t * nr + spot
        return div(g, S2), rcopy(
            b2s.at[t], out2_in.at[pl.ds(rem(g, S2) * sub, sub)],
            o2_send.at[t], o2_recv.at[rem(g, S2)], holder_of(div(g, S2)),
        )

    def stays(d):
        return lax.min(lax.abs(d - prow) + abroad, 1) == 0

    def send_out(n, copy, src, dst):
        def go(a):
            d, cp = copy(a)

            @pl.when(jnp.logical_not(stays(d)))
            def _():
                cp.start()

            @pl.when(stays(d))
            def _():
                at = rem(a * nr + spot, n) * sub
                dst[pl.ds(pl.multiple_of(at, sub), sub), :] = src[a]

        each(n, go)

    def take_out(n, src, dst, send, recv):
        def go(a):
            m = rem(prow * n + a, nr)

            @pl.when(lax.min(lax.abs(m - spot) + abroad, 1) == 1)
            def _():
                rcopy(
                    src.at[0], dst.at[pl.ds(a * sub, sub)], send.at[a], recv.at[a],
                    device(x, home, div(m, nk), rem(m, nk)),
                ).wait_recv()

        each(n, go)

    def done_out(n, copy):
        def go(a):
            d, cp = copy(a)

            @pl.when(jnp.logical_not(stays(d)))
            def _():
                cp.wait_send()

        each(n, go)

    send_out(S1, o1_copy, acc1, out1_in)

    def x_copy(g, cs):
        return rcopy(part.at[:, 1 - core, :, cs], sibpart.at[:, :, cs], x_send.at[g], x_recv.at[g], sibling)

    def s_copy(g, cs, k):
        d = rem(zeta + k + 1, nz)
        return rcopy(
            comb.at[d, :, cs], sums.at[zeta, :, cs], s_send.at[g, k], s_recv.at[g, k], device(x, y, virtual(d), core)
        )

    spans = [pl.ds(0, B), pl.ds(B, 2 * B), pl.ds(3 * B, 2 * B)]

    def combine(g):
        cs = spans[g]
        x_copy(g, cs).wait_recv()
        comb[:, :, cs] = part[:, core, :, cs] + sibpart[:, :, cs]
        for k in range(nz - 1):
            s_copy(g, cs, k).start()

    node = node_of(x, y)
    for a in range(S1):
        low1[a * sub : (a + 1) * sub, :] = l1[pl.ds(pl.multiple_of(a * B + spot * sub, sub), sub), :]
    square = mm_t(low1[...], acc1[...].reshape(S1 * sub, B))
    part[:, :, :, 0:B] = square.reshape(nz, nk, sub, B)
    x_copy(0, spans[0]).start()
    pivot1 = lg[me, gathered : gathered + sub, :]

    for ch in range(2):
        for t in range(S2):
            low2[t * sub : (t + 1) * sub, :] = l2[ch, pl.ds(pl.multiple_of(t * B + spot * sub, sub), sub), :]
        pos = []
        for t in range(S2):
            want = sets_two[2 * node + ch, t]
            at = 0
            for s in range(S1):
                at = at + s * (1 - lax.min(lax.abs(sets_one[node, s] - want), 1))
            pos.append(lax.min(at, S1 - 1))
        total = mm(grid[pos[0]], l2[ch, 0:B, :])
        for t in range(1, S2):
            total = total + mm(grid[pos[t]], l2[ch, t * B : (t + 1) * B, :])
        acc2[...] = total.reshape(acc2.shape)
        for t in range(S2):
            dir2[t * sub : (t + 1) * sub, :] = acc2[pos[t]]
            upper[t * sub : (t + 1) * sub, :] = acc1[pos[t]]
        pc = pf[ch]
        u = upper[...]
        l2c = low2[...]
        b2 = -(dir2[...] + mm(u, pc))
        b2s[:, :, ch * B : (ch + 1) * B] = b2.reshape(S2, sub, B)
        cross = mm_t(u, l2c)
        inner = cross - mm(part[:, :, :, 0:B].reshape(B, B), pc)
        mine = pf[ch, pl.ds(pl.multiple_of(me * sub, sub), sub), :]
        last = mm_t(pc, inner) - mm_t(l2c, b2) + mm_t(mine, mm(pivot1, pc))
        o = B + 2 * ch * B
        part[:, :, :, o : o + B] = cross.reshape(nz, nk, sub, B)
        part[:, :, :, o + B : o + 2 * B] = last.reshape(nz, nk, sub, B)
        x_copy(ch + 1, spans[ch + 1]).start()
        combine(ch)

    combine(2)
    send_out(S2, o2_copy, b2s, out2_in)

    for g in range(3):
        for k in range(nz - 1):
            s_copy(g, spans[g], k).wait_recv()

    total = comb[zeta]
    for k in range(1, nz):
        total = total + sums[rem(zeta + k, nz)]
    corner = pivot1 - total[:, 0:B]
    fin[:, 0:B] = corner
    for ch in range(2):
        o = B + 2 * ch * B
        p2 = gathered + sub + ch * sub
        fin[:, (1 + ch) * B : (2 + ch) * B] = -(mm(corner, pf[ch]) + total[:, o : o + B])
        fin[:, (3 + ch) * B : (4 + ch) * B] = lg[me, p2 : p2 + sub, :] + total[:, o + B : o + 2 * B]

    back = rcopy(fin, fin_in, back_sem.at[0], back_sem.at[1], holder)

    @pl.when(away)
    def _():
        back.start()

    take_out(S1, acc1, out1_in, o1_send, o1_recv)
    take_out(S2, b2s, out2_in, o2_send, o2_recv)

    @pl.when(away)
    def _():
        back.wait_recv()

    @pl.when(jnp.logical_not(away))
    def _():
        fin_in[...] = fin[...]

    @pl.when(away)
    def _():
        for piece in range(2):
            swap_copy(piece).wait_send()
        back.wait_send()

    for i in range(nbr):
        each(nr - 1, lambda k: a_copy(k, i).wait_send())
        for k in range(nc - 1):
            b_copy(k, i).wait_send()
    for k in range(nc - 1):
        c_copy(k).wait_send()
    for way, piece in STREAMS:
        for s in range(length(way, piece)):
            ring_copy(way, piece, s).wait_send()
            sib_copy(way, piece, s + 1).wait_send()
    for piece in range(2):
        sib_copy(1, piece, 0).wait_send()
    for g in range(3):
        x_copy(g, spans[g]).wait_send()
        for k in range(nz - 1):
            s_copy(g, spans[g], k).wait_send()
    done_out(S1, o1_copy)
    done_out(S2, o2_copy)


def deliver(one, two, rest, below_one, corner_one, below_two, beside, corner_two):
    B = one.shape[1]
    below_one[...] = one[...]
    below_two[...] = two[...]
    corner_one[...] = rest[:, 0:B]
    beside[...] = rest[:, B : 3 * B]
    corner_two[...] = rest[:, 3 * B : 5 * B]


def on_device(top, panel_one, panel_two, parent, pivot_one, pivot_two, sets_one, sets_two):
    nx, ny, nzh, nzl, nk = DIMS
    nz = nzh * nzl
    nr = nz * nk
    nc = nx * ny
    S1 = sets_one.shape[1]
    S2 = sets_two.shape[1]
    B = panel_one.shape[1]
    sub = B // nr
    H = max(B // 128, 1)
    LN = B // H
    nbr, nbc = top.shape[0] // B, top.shape[1] // B
    npc = S1 * S1 * H
    share1, share2 = S1 * sub, S2 * sub
    gathered = share1 + 2 * share2 + 2 * sub
    whole = gathered + 3 * sub
    steps = nz // 2
    cfg = (B, S1, S2)
    top = top.reshape(nbr, nr, sub, nbc, H, LN)
    vmem = pl.BlockSpec(memory_space=pltpu.VMEM)
    smem = pl.BlockSpec(memory_space=pltpu.SMEM)
    V = lambda *s: pltpu.VMEM(s, F32)
    D = lambda *s: pltpu.SemaphoreType.DMA(s)
    out = lambda *s: jax.ShapeDtypeStruct(s, F32)
    one, two, rest = pl.pallas_call(
        functools.partial(kernel, cfg),
        out_shape=(out(share1, B), out(share2, 2 * B), out(sub, 5 * B)),
        in_specs=[smem, smem] + [vmem] * 6,
        out_specs=(vmem,) * 3,
        scratch_shapes=[
            V(nbr, nr, sub, nbc, H, LN),
            V(nc * nr * nbr, nbc, H, LN),
            V(nc, npc, LN),
            V(nc * npc, LN),
            V(S1, share1, B),
            V(whole, B),
            V(nr, whole, B),
            V(S1 * B, B),
            V(2, S2 * B, B),
            V(2, B, B),
            V(S1, sub, B),
            V(S1, sub, B),
            V(share1, B),
            V(share2, B),
            V(share2, B),
            V(share2, B),
            V(S2, sub, 2 * B),
            V(nz, nk, sub, 5 * B),
            V(nz, sub, 5 * B),
            V(nz, sub, 5 * B),
            V(nz, sub, 5 * B),
            V(sub, 5 * B),
            D(2, 2),
            D(nbr, nr - 1), D(nbr, nr - 1), D(nbr, nc), D(nbr, nc), D(nc), D(nc),
            D(2, 2, steps), D(2, 2, steps), D(2, 2, steps + 1), D(2, 2, steps + 1), D(2 + nbr),
            D(3), D(3), D(3, nz - 1), D(3, nz - 1), D(S1), D(S1), D(S2), D(S2), D(2),
        ],
        compiler_params=pltpu.CompilerParams(
            collective_id=0, has_side_effects=True, vmem_limit_bytes=56 * 1024 * 1024
        ),
    )(sets_one, sets_two, top, panel_one, panel_two, parent, pivot_one, pivot_two)
    return pl.pallas_call(
        deliver,
        out_shape=(out(share1, B), out(sub, B), out(share2, 2 * B), out(sub, 2 * B), out(sub, 2 * B)),
        in_specs=[vmem] * 3,
        out_specs=(vmem,) * 5,
    )(one, two, rest)


def solution(mesh):
    spec = P("prow", "pcol")
    return jax.shard_map(
        on_device,
        mesh=mesh,
        in_specs=(spec,) * 6 + (P(), P()),
        out_specs=(spec,) * 5,
        check_vma=False,
    )
```
